32 devices in a mesh: groups: 2 (over y), row: 4 (over z), col: 4 (over x, core).
Axes of the slice: x: 2, y: 2, z: 4, core: 2. Of those that a mesh axis runs over, the one named last changes fastest.
Arguments:
- wavefunction: bfloat16 [2048, 4096], P(('groups', 'row'), 'col'), parts along dimension 0, may hold values from -18 to 18, as said below
- left_ops: bfloat16 [8, 8, 256, 256], P(None, ('groups', 'row')), parts along dimension 1, may hold values from -0.125 to 0.125
- right_ops: bfloat16 [8, 32, 256, 256], P(None, ('groups', 'col')), parts along dimension 1, may hold values from -0.375 to 0.375
- left_dest: int32 [8, 8], P(None, 'groups'), parts along dimension 1, may hold values from 0 to 3
- right_src: int32 [8, 32], P(None, 'groups'), parts along dimension 1, may hold values from 0 to 15
- left_sizes: int32 [8], P('groups'), parts along dimension 0, may hold values from 64 to 256, as said below
- right_sizes: int32 [32], P('groups'), parts along dimension 0, may hold values from 64 to 256, as said below
Outputs:
- first_product: bfloat16 [2048, 4096], P(('groups', 'row'), 'col'), parts along dimension 0
- second_product: bfloat16 [2048, 4096], P(('groups', 'row'), 'col'), parts along dimension 0
The draws below stay inside these ranges and needn't reach their ends.
There are 2 independent parts, one for each index of `groups`. The reference program is written for one: setup_inputs(seed, part) draws one part's arguments, and reference() takes and returns one part's arrays. A program takes and returns all parts, laid end to end along the dimension named above; each array names one. Nothing has to cross between parts.
Inputs may be any that keep to these rules, and one draw needn't show every extreme that they name: `wavefunction`: entries of order one. `left_sizes`: each left sector size is between 64 and 256; both ends are taken. `right_sizes`: each right sector size is between 64 and 256; both ends are taken.
All inputs are finite; a program needn't handle non-finite values.
Results may differ from the reference program's by a relative error of at most 0.02.
Values may be sent and summed in bfloat16 or wider, within the bound.
No kernel may reach another device: no remote copies, remote signals or barrier semaphores. Data moves between devices by JAX's collectives and lax.ppermute only.
A program may use at most 64 MiB of HBM per device.

```python
import jax
import jax.numpy as jnp
from jax import lax

TILE = 256
TERMS = 8
NBL = 4
NBR = 16
NL = 1024
NR = 4096


def sector_sizes(key, count):
    first_key, second_key = jax.random.split(key)
    sizes = jax.random.randint(first_key, (count,), TILE // 4, TILE + 1)
    widest = jax.random.randint(second_key, (), 0, count)
    narrow = (widest + 1) % count
    places = jnp.arange(count)
    sizes = jnp.where(places == widest, TILE, sizes)
    sizes = jnp.where(places == narrow, TILE // 4, sizes)
    return sizes.astype(jnp.int32)


def draw_left_sizes(key, part):
    key = jax.random.fold_in(key, 11)
    return sector_sizes(key, NBL)


def draw_right_sizes(key, part):
    key = jax.random.fold_in(key, 23)
    return sector_sizes(key, NBR)


def draw_wavefunction(key, part):
    key = jax.random.fold_in(key, 37)
    block_index = (jnp.arange(NL) // TILE).astype(jnp.float32)
    values = jnp.clip(jax.random.normal(key, (NL, NR), jnp.float32), -6.0, 6.0)
    amplitude = 1.0 + 2.0 * block_index / (NBL - 1)
    return (values * amplitude[:, None]).astype(jnp.bfloat16)


def with_ends(values, stream_key, smallest, largest):
    shape = values.shape
    index_at = [jax.random.randint(jax.random.fold_in(stream_key, axis), (), 0, shape[axis]) for axis in range(len(shape))]
    values = values.at[tuple(index_at)].set(smallest)
    longest = shape.index(max(shape))
    index_at[longest] = (index_at[longest] + 1) % shape[longest]
    return values.at[tuple(index_at)].set(largest)


def shard_levels(key, extent, pieces, least, top_value):
    factor_of = 1.0
    for dim, blocks in pieces:
        draws = jax.random.uniform(jax.random.fold_in(jax.random.fold_in(key, 6), dim), (blocks,), jnp.float32, least / len(pieces), top_value / len(pieces))
        factor_of = factor_of * jnp.repeat(jnp.exp(draws), extent[dim] // blocks).reshape((-1,) + (1,) * (len(extent) - 1 - dim))
    return factor_of


def normal_values(own_key, shape, width, most, cuts=(), dtype=jnp.bfloat16):
    entries = width * jax.random.normal(own_key, shape, jnp.float32)
    if cuts:
        entries = entries * shard_levels(own_key, shape, cuts, -0.22, 0.18)
    return jnp.clip(entries, -most, most).astype(dtype)


def setup_inputs(seed: int = 0, part: int = 0) -> dict:
    key_list = jax.random.split(jax.random.key(seed), 8)
    part_splits = jax.random.split(jax.random.fold_in(key_list[7], part), 8)
    wavefunction = draw_wavefunction(jax.random.fold_in(jax.random.fold_in(key_list[7], part), 71), part)
    left_ops = normal_values(part_splits[1], (TERMS, NBL, TILE, TILE), (TILE * TERMS) ** -0.5, 0.125, ((1, 4),))
    right_ops = normal_values(part_splits[2], (TERMS, NBR, TILE, TILE), TILE ** -0.5, 0.375, ((1, 4),))
    left_dest = with_ends(jax.random.randint(part_splits[3], (TERMS, NBL), 0, NBL), jax.random.fold_in(part_splits[3], 1), 0, NBL - 1).astype(jnp.int32)
    right_src = with_ends(jax.random.randint(part_splits[4], (TERMS, NBR), 0, NBR), jax.random.fold_in(part_splits[4], 1), 0, NBR - 1).astype(jnp.int32)
    left_sizes = draw_left_sizes(jax.random.fold_in(jax.random.fold_in(key_list[7], part), 71), part)
    right_sizes = draw_right_sizes(jax.random.fold_in(jax.random.fold_in(key_list[7], part), 71), part)
    return {"wavefunction": wavefunction, "left_ops": left_ops, "right_ops": right_ops, "left_dest": left_dest, "right_src": right_src, "left_sizes": left_sizes, "right_sizes": right_sizes}


def build_mask(left_sizes, right_sizes):
    offsets = jnp.arange(TILE)
    left_rows = (offsets[None, :] < left_sizes[:, None]).reshape(-1)
    right_cols = (offsets[None, :] < right_sizes[:, None]).reshape(-1)
    return (left_rows[:, None] & right_cols[None, :]).astype(jnp.bfloat16)

def apply_hamiltonian(vector, left_ops, right_ops, left_dest, right_src):
    right_full = right_ops.astype(jnp.float32)

    def one_block(total, block):
        rows = lax.dynamic_slice_in_dim(vector, block * TILE, TILE, 0).astype(jnp.float32)
        blocks = rows.reshape(TILE, NBR, TILE)
        chosen = jnp.take(blocks, right_src, axis=1)
        inner_terms = jnp.einsum('rtjc,tjdc->trjd', chosen, right_full).astype(jnp.bfloat16)
        inner_terms = lax.optimization_barrier(inner_terms).astype(jnp.float32).reshape(TERMS, TILE, NR)
        left_block = lax.dynamic_index_in_dim(left_ops, block, 1, keepdims=False).astype(jnp.float32)
        contrib = jnp.einsum('tab,tbn->tan', left_block, inner_terms)
        targets = lax.dynamic_index_in_dim(left_dest, block, 1, keepdims=False)
        onehot = (targets[:, None] == jnp.arange(NBL)[None, :]).astype(jnp.float32)
        partial_sum = jnp.einsum('tk,tan->kan', onehot, contrib).reshape(NL, NR).astype(jnp.bfloat16)
        partial_sum = lax.optimization_barrier(partial_sum).astype(jnp.float32)
        return (total + partial_sum, None)
    total, unused = lax.scan(one_block, jnp.zeros((NL, NR), jnp.float32), jnp.arange(NBL).astype(jnp.int32))
    return total

def reference(wavefunction, left_ops, right_ops, left_dest, right_src, left_sizes, right_sizes):
    valid_mask = build_mask(left_sizes, right_sizes)
    mask_float = valid_mask.astype(jnp.float32)
    masked = wavefunction * valid_mask
    masked_float = masked.astype(jnp.float32)
    image = apply_hamiltonian(masked, left_ops, right_ops, left_dest, right_src) * mask_float
    norm_total = jnp.sum(masked_float * masked_float)
    correlation_total = jnp.sum(masked_float * image)
    scale = lax.rsqrt(norm_total / (NL * NR) + 1e-06)
    theta = correlation_total / norm_total
    first_product = (image * scale).astype(jnp.bfloat16)
    residual = ((image - theta * masked_float) * scale).astype(jnp.bfloat16)
    second_product = (apply_hamiltonian(residual, left_ops, right_ops, left_dest, right_src) * mask_float).astype(jnp.bfloat16)
    return (first_product, second_product)
```

```python
import functools

import jax
import jax.numpy as jnp
from jax import lax
from jax.experimental import pallas as pl
from jax.experimental.pallas import tpu as pltpu
from jax.sharding import PartitionSpec as P

CHUNKS = 2


def swap(axis, bit):
    size = lax.axis_size(axis)
    return [(place, place ^ bit) for place in range(size)]


def bits_of(size):
    count = size.bit_length() - 1
    assert 1 << count == size
    return count


def reverse_bits(value, count):
    out = jnp.zeros_like(value)
    for bit in range(count):
        out = out | (((value >> bit) & 1) << (count - 1 - bit))
    return out


def product_kernel(first, piece_count, local, slots, src_ref, dest_ref, *refs):
    pieces = refs[:piece_count]
    left_ref, right_ref, out_ref, blocks, total = refs[piece_count:]
    tile = left_ref.shape[1]
    terms = left_ref.shape[0]
    step = pl.program_id(0)

    @pl.when(step == 0)
    def _():
        for piece in range(piece_count):
            for place in range(local):
                blocks[piece * local + place] = pieces[piece][:, place * tile:(place + 1) * tile]

    total[...] = jnp.zeros_like(total)
    for term in range(terms):
        rows = blocks[src_ref[term, first + step]]
        inner = lax.dot_general(
            rows, right_ref[term, 0], (((1,), (1,)), ((), ())), preferred_element_type=jnp.float32
        ).astype(jnp.bfloat16)
        total[dest_ref[term]] += jnp.dot(left_ref[term], inner, preferred_element_type=jnp.float32)
    out_ref[...] = total[...].astype(jnp.bfloat16)


def products(pieces, left, right, source, target, slots, first, count):
    terms, tile = left.shape[:2]
    local = right.shape[1]
    whole = lambda step, *tables: (0, 0)
    return pl.pallas_call(
        functools.partial(product_kernel, first, len(pieces), local, slots),
        grid_spec=pltpu.PrefetchScalarGridSpec(
            num_scalar_prefetch=2,
            grid=(count,),
            in_specs=[pl.BlockSpec((tile, local * tile), whole) for _ in pieces] + [
                pl.BlockSpec((terms, tile, tile), lambda step, *tables: (0, 0, 0)),
                pl.BlockSpec((terms, 1, tile, tile), lambda step, *tables: (0, first + step, 0, 0)),
            ],
            out_specs=pl.BlockSpec((slots, tile, tile), lambda step, *tables: (0, 0, step)),
            scratch_shapes=[
                pltpu.VMEM((len(pieces) * local, tile, tile), jnp.bfloat16),
                pltpu.VMEM((slots, tile, tile), jnp.float32),
            ],
        ),
        out_shape=jax.ShapeDtypeStruct((slots, tile, count * tile), jnp.bfloat16),
        compiler_params=pltpu.CompilerParams(vmem_limit_bytes=40 * 1024 * 1024),
        cost_estimate=pl.CostEstimate(
            flops=4 * terms * count * tile**3, bytes_accessed=terms * (count + 1) * tile * tile * 2, transcendentals=0
        ),
    )(source, target, *pieces, left, right)


def on_device(wavefunction, left_ops, right_ops, left_dest, right_src, left_sizes, right_sizes):
    tile = left_ops.shape[2]
    local = right_ops.shape[1]
    row_count, col_count = lax.axis_size("row"), lax.axis_size("col")
    row_bits, col_bits = bits_of(row_count), bits_of(col_count)
    entry_count = wavefunction.shape[0] * row_count * wavefunction.shape[1] * col_count
    row, col = lax.axis_index("row"), lax.axis_index("col")
    dest_here = lax.dynamic_index_in_dim(left_dest, row, 1, keepdims=False)
    source_here = lax.dynamic_slice_in_dim(right_src, col * local, local, 1)
    left_size = lax.dynamic_index_in_dim(left_sizes, row, 0, keepdims=False)
    right_here = lax.dynamic_slice_in_dim(right_sizes, col * local, local, 0)
    offsets = jnp.arange(tile)
    row_valid = offsets < left_size
    col_valid = (offsets[None, :] < right_here[:, None]).reshape(-1)
    valid = row_valid[:, None] & col_valid[None, :]
    left_here = left_ops[:, 0]
    source = ((source_here // local) ^ col) * local + source_here % local
    target = reverse_bits(dest_here ^ row, row_bits)

    def gather(part):
        pieces = {0: part}
        for bit in reversed(range(col_bits)):
            for place in list(pieces):
                pieces[place | (1 << bit)] = lax.ppermute(pieces[place], "col", swap("col", 1 << bit))
        return [pieces[place] for place in range(col_count)]

    def scatter_sum(sums):
        for bit in range(row_bits):
            half = sums.shape[0] // 2
            arrived = lax.ppermute(sums[half:], "row", swap("row", 1 << bit))
            total = sums[:half].astype(jnp.float32) + arrived.astype(jnp.float32)
            sums = total.astype(jnp.bfloat16) if bit < row_bits - 1 else total
        return sums[0]

    def apply_h(pieces):
        step = local // CHUNKS
        out = []
        for first in range(0, local, step):
            sums = products(pieces, left_here, right_ops, source, target, row_count, first, step)
            out.append(scatter_sum(sums))
        return out

    masked = jnp.where(valid, wavefunction, 0)
    masked_float = masked.astype(jnp.float32)
    width = wavefunction.shape[1] // CHUNKS
    parts = apply_h(gather(masked))
    parts = [jnp.where(valid[:, i * width:(i + 1) * width], part, 0.0) for i, part in enumerate(parts)]
    image_pieces = [gather(part.astype(jnp.bfloat16)) for part in parts]
    image_pieces = [jnp.concatenate(several, 1) for several in zip(*image_pieces)]
    image = jnp.concatenate(parts, 1)
    own = jnp.stack([jnp.sum(masked_float * masked_float), jnp.sum(masked_float * image)])
    sums = jnp.sum(lax.all_gather(jnp.broadcast_to(own[:, None], (2, 128)), ("row", "col")), 0)
    norm_total, correlation_total = sums[0, 0], sums[1, 0]
    scale = lax.rsqrt(norm_total / entry_count + 1e-06)
    theta = correlation_total / norm_total
    first_product = (image * scale).astype(jnp.bfloat16)
    again = jnp.concatenate(apply_h(image_pieces), 1)
    second_product = jnp.where(valid, (again - theta * image) * scale, 0.0).astype(jnp.bfloat16)
    return (first_product, second_product)


def solution(mesh):
    placed = (
        P(("groups", "row"), "col"),
        P(None, ("groups", "row"), None, None),
        P(None, ("groups", "col"), None, None),
        P(None, "groups"),
        P(None, "groups"),
        P("groups"),
        P("groups"),
    )
    return jax.shard_map(
        on_device,
        mesh=mesh,
        in_specs=placed,
        out_specs=(P(("groups", "row"), "col"), P(("groups", "row"), "col")),
        check_vma=False,
    )
```

```python
import functools

import jax
import jax.numpy as jnp
from jax import lax
from jax.experimental import pallas as pl
from jax.experimental.pallas import tpu as pltpu
from jax.sharding import PartitionSpec as P

CHUNKS = 2


def swap(axis, bit):
    size = lax.axis_size(axis)
    return [(place, place ^ bit) for place in range(size)]


def bits_of(size):
    count = size.bit_length() - 1
    assert 1 << count == size
    return count


def reverse_bits(value, count):
    out = jnp.zeros_like(value)
    for bit in range(count):
        out = out | (((value >> bit) & 1) << (count - 1 - bit))
    return out


def product_kernel(first, piece_count, local, slots, src_ref, dest_ref, *refs):
    pieces = refs[:piece_count]
    left_ref, right_ref, out_ref, blocks, total = refs[piece_count:]
    tile = left_ref.shape[1]
    terms = left_ref.shape[0]
    step = pl.program_id(0)

    @pl.when(step == 0)
    def _():
        per_piece = local * tile // pieces[0].shape[1]
        for place in range(len(pieces) // per_piece * local):
            held = pieces[place * per_piece // local]
            at = place % (local // per_piece) * tile
            blocks[place] = held[:, at:at + tile]

    total[...] = jnp.zeros_like(total)
    for term in range(terms):
        rows = blocks[src_ref[term, first + step]]
        inner = lax.dot_general(
            rows, right_ref[term, 0], (((1,), (1,)), ((), ())), preferred_element_type=jnp.float32
        ).astype(jnp.bfloat16)
        total[dest_ref[term]] += jnp.dot(left_ref[term], inner, preferred_element_type=jnp.float32)
    out_ref[...] = total[...].astype(jnp.bfloat16)


def products(pieces, left, right, source, target, slots, first, count):
    terms, tile = left.shape[:2]
    local = right.shape[1]
    whole = lambda step, *tables: (0, 0)
    return pl.pallas_call(
        functools.partial(product_kernel, first, len(pieces), local, slots),
        grid_spec=pltpu.PrefetchScalarGridSpec(
            num_scalar_prefetch=2,
            grid=(count,),
            in_specs=[pl.BlockSpec(piece.shape, whole) for piece in pieces] + [
                pl.BlockSpec((terms, tile, tile), lambda step, *tables: (0, 0, 0)),
                pl.BlockSpec((terms, 1, tile, tile), lambda step, *tables: (0, first + step, 0, 0)),
            ],
            out_specs=pl.BlockSpec((slots, tile, tile), lambda step, *tables: (0, 0, step)),
            scratch_shapes=[
                pltpu.VMEM((sum(piece.shape[1] for piece in pieces) // tile, tile, tile), jnp.bfloat16),
                pltpu.VMEM((slots, tile, tile), jnp.float32),
            ],
        ),
        out_shape=jax.ShapeDtypeStruct((slots, tile, count * tile), jnp.bfloat16),
        compiler_params=pltpu.CompilerParams(vmem_limit_bytes=56 * 1024 * 1024),
        cost_estimate=pl.CostEstimate(
            flops=4 * terms * count * tile**3, bytes_accessed=terms * (count + 1) * tile * tile * 2, transcendentals=0
        ),
    )(source, target, *pieces, left, right)


def on_device(wavefunction, left_ops, right_ops, left_dest, right_src, left_sizes, right_sizes):
    tile = left_ops.shape[2]
    local = right_ops.shape[1]
    row_count, col_count = lax.axis_size("row"), lax.axis_size("col")
    row_bits, col_bits = bits_of(row_count), bits_of(col_count)
    entry_count = wavefunction.shape[0] * row_count * wavefunction.shape[1] * col_count
    row, col = lax.axis_index("row"), lax.axis_index("col")
    dest_here = lax.dynamic_index_in_dim(left_dest, row, 1, keepdims=False)
    source_here = lax.dynamic_slice_in_dim(right_src, col * local, local, 1)
    left_size = lax.dynamic_index_in_dim(left_sizes, row, 0, keepdims=False)
    right_here = lax.dynamic_slice_in_dim(right_sizes, col * local, local, 0)
    offsets = jnp.arange(tile)
    row_valid = offsets < left_size
    col_valid = (offsets[None, :] < right_here[:, None]).reshape(-1)
    valid = row_valid[:, None] & col_valid[None, :]
    left_here = left_ops[:, 0]
    source = ((source_here // local) ^ col) * local + source_here % local
    target = reverse_bits(dest_here ^ row, row_bits)

    def gather(part):
        pieces = {0: part}
        for bit in reversed(range(col_bits)):
            for place in list(pieces):
                pieces[place | (1 << bit)] = lax.ppermute(pieces[place], "col", swap("col", 1 << bit))
        return [pieces[place] for place in range(col_count)]

    def scatter_sum(sums):
        for bit in range(row_bits):
            half = sums.shape[0] // 2
            arrived = lax.ppermute(sums[half:], "row", swap("row", 1 << bit))
            total = sums[:half].astype(jnp.float32) + arrived.astype(jnp.float32)
            sums = total.astype(jnp.bfloat16) if bit < row_bits - 1 else total
        return sums[0]

    def apply_h(pieces):
        step = local // CHUNKS
        out = []
        for first in range(0, local, step):
            sums = products(pieces, left_here, right_ops, source, target, row_count, first, step)
            out.append(scatter_sum(sums))
        return out

    masked = jnp.where(valid, wavefunction, 0)
    masked_float = masked.astype(jnp.float32)
    width = wavefunction.shape[1] // CHUNKS
    parts = apply_h(gather(masked))
    parts = [jnp.where(valid[:, i * width:(i + 1) * width], part, 0.0) for i, part in enumerate(parts)]
    image_pieces = [gather(part.astype(jnp.bfloat16)) for part in parts]
    image_pieces = [part for several in zip(*image_pieces) for part in several]
    image = jnp.concatenate(parts, 1)
    own = jnp.stack([jnp.sum(masked_float * masked_float), jnp.sum(masked_float * image)])
    sums = jnp.broadcast_to(own[:, None], (2, 128))
    for axis, bits in (("col", col_bits), ("row", row_bits)):
        for bit in range(bits):
            sums = sums + lax.ppermute(sums, axis, swap(axis, 1 << bit))
    norm_total, correlation_total = sums[0, 0], sums[1, 0]
    scale = lax.rsqrt(norm_total / entry_count + 1e-06)
    theta = correlation_total / norm_total
    first_product = (image * scale).astype(jnp.bfloat16)
    again = jnp.concatenate(apply_h(image_pieces), 1)
    second_product = jnp.where(valid, (again - theta * image) * scale, 0.0).astype(jnp.bfloat16)
    return (first_product, second_product)


def solution(mesh):
    placed = (
        P(("groups", "row"), "col"),
        P(None, ("groups", "row"), None, None),
        P(None, ("groups", "col"), None, None),
        P(None, "groups"),
        P(None, "groups"),
        P("groups"),
        P("groups"),
    )
    return jax.shard_map(
        on_device,
        mesh=mesh,
        in_specs=placed,
        out_specs=(P(("groups", "row"), "col"), P(("groups", "row"), "col")),
        check_vma=False,
    )
```

```python
import functools

import jax
import jax.numpy as jnp
from jax import lax
from jax.experimental import pallas as pl
from jax.experimental.pallas import tpu as pltpu
from jax.sharding import PartitionSpec as P

CHUNKS = 2
MIB = 1024 * 1024
VMEM = pl.BlockSpec(memory_space=pltpu.VMEM)
SMEM = pl.BlockSpec(memory_space=pltpu.SMEM)


def bits_of(size):
    count = size.bit_length() - 1
    assert 1 << count == size
    return count


def swap(axis, bit):
    return [(place, place ^ bit) for place in range(lax.axis_size(axis))]


def leads(row):
    return (row ^ (row >> 1)) & 1


def leader_swap(bit):
    rows, cols = lax.axis_size("row"), lax.axis_size("col")
    pairs = []
    for row in range(rows):
        for col in range(cols):
            if leads(row):
                pair = (row >> 1) ^ bit
                there = (2 * pair if leads(2 * pair) else 2 * pair + 1, col)
            else:
                there = (row, col ^ 1)
            pairs.append((row * cols + col, there[0] * cols + there[1]))
    return pairs


def reverse_bits(value, count):
    out = 0
    for bit in range(count):
        out = out | (((value >> bit) & 1) << (count - 1 - bit))
    return out


def valid_block(shape, left_sizes, right_sizes, row, block):
    return (lax.broadcasted_iota(jnp.int32, shape, 0) < left_sizes[row]) & (
        lax.broadcasted_iota(jnp.int32, shape, 1) < right_sizes[block]
    )


def fold(values):
    rows = jnp.sum(values.reshape(-1, 8, values.shape[1]), 0)
    return sum(rows[:, at:at + 128] for at in range(0, rows.shape[1], 128))


def prepare_kernel(left_sizes, right_sizes, wavefunction, masked):
    local, tile = masked.shape[:2]
    row, col = lax.axis_index("row"), lax.axis_index("col")
    for place in range(local):
        valid = valid_block((tile, tile), left_sizes, right_sizes, row, col * local + place)
        block = wavefunction[:, place * tile:(place + 1) * tile].astype(jnp.float32)
        masked[place] = jnp.where(valid, block, 0.0).astype(masked.dtype)


def product_kernel(first, count, piece_count, row_count, source, target, *refs):
    pieces, refs = refs[:2 * piece_count], refs[2 * piece_count:]
    left, right, refs = refs[:2], refs[2], refs[3:]
    outs, (blocks, inner, total) = refs[:row_count], refs[row_count:]
    terms, local, tile = right.shape[:3]
    row, col = lax.axis_index("row"), lax.axis_index("col")
    for slot in range(2):
        at = 0
        for piece in pieces[slot * piece_count:(slot + 1) * piece_count]:
            for place in range(piece.shape[0]):
                blocks[at, slot * tile:(slot + 1) * tile] = piece[place]
                at += 1

    def one_block(step, carry):
        place = first + step
        for term in range(terms):
            wanted = source[term, col * local + place]
            held = lax.bitwise_xor(lax.div(wanted, local), col) * local + lax.rem(wanted, local)
            inner[term] = lax.dot_general(
                blocks[held], right[term, place], (((1,), (1,)), ((), ())), preferred_element_type=jnp.float32
            ).astype(jnp.bfloat16)
        total[...] = jnp.zeros_like(total)
        for term in range(terms):
            for slot in range(2):
                to = target[term, row ^ slot]
                to_slot = 2 * reverse_bits((to >> 1) ^ (row >> 1), bits_of(row_count) - 1) + 1 - leads(to)
                total[to_slot] += jnp.dot(
                    left[slot][term], inner[term, slot * tile:(slot + 1) * tile], preferred_element_type=jnp.float32
                )
        for slot in range(row_count):
            outs[slot][step] = total[slot].astype(outs[slot].dtype)
        return carry

    lax.fori_loop(0, count, one_block, 0)


def products(pieces, left, right, source, target, row_count, first, count):
    terms, local, tile = right.shape[:3]
    pieces = [piece for row_pieces in pieces for piece in row_pieces]
    blocks = sum(piece.shape[0] for piece in pieces) // 2
    return pl.pallas_call(
        functools.partial(product_kernel, first, count, len(pieces) // 2, row_count),
        in_specs=[SMEM, SMEM] + [VMEM] * (len(pieces) + 3),
        out_specs=[VMEM] * row_count,
        out_shape=[
            jax.ShapeDtypeStruct((count, tile, tile), jnp.float32 if slot < 2 else jnp.bfloat16)
            for slot in range(row_count)
        ],
        scratch_shapes=[
            pltpu.VMEM((blocks, 2 * tile, tile), jnp.bfloat16),
            pltpu.VMEM((terms, 2 * tile, tile), jnp.bfloat16),
            pltpu.VMEM((row_count, tile, tile), jnp.float32),
        ],
        compiler_params=pltpu.CompilerParams(vmem_limit_bytes=30 * MIB),
        cost_estimate=pl.CostEstimate(flops=8 * terms * count * tile**3, bytes_accessed=8 * MIB, transcendentals=0),
    )(source, target, *pieces, *left, right)


def combine_kernel(slot, first, left_sizes, right_sizes, kept, arrived, masked, image, rounded, stats):
    count, tile = kept.shape[:2]
    row, col = lax.axis_index("row") ^ slot, lax.axis_index("col")
    norm = correlation = jnp.zeros((8, 128), jnp.float32)
    for step in range(count):
        valid = valid_block((tile, tile), left_sizes, right_sizes, row, col * masked.shape[0] + first + step)
        value = jnp.where(valid, kept[step] + arrived[step].astype(jnp.float32), 0.0)
        image[step] = value
        rounded[step] = value.astype(jnp.bfloat16)
        vector = masked[first + step].astype(jnp.float32)
        norm += fold(vector * vector)
        correlation += fold(vector * value)
    stats[0] = norm
    stats[1] = correlation


def combine(slot, first, left_sizes, right_sizes, kept, arrived, masked):
    return pl.pallas_call(
        functools.partial(combine_kernel, slot, first),
        in_specs=[SMEM, SMEM, VMEM, VMEM, VMEM],
        out_specs=[VMEM] * 3,
        out_shape=[
            jax.ShapeDtypeStruct(kept.shape, jnp.float32),
            jax.ShapeDtypeStruct(kept.shape, jnp.bfloat16),
            jax.ShapeDtypeStruct((2, 8, 128), jnp.float32),
        ],
        cost_estimate=pl.CostEstimate(flops=8 * kept.size, bytes_accessed=10 * kept.size, transcendentals=0),
    )(left_sizes, right_sizes, kept, arrived, masked)


def scale_theta(entry_count, stats):
    norm, correlation = jnp.sum(stats[0]), jnp.sum(stats[1])
    norm = jnp.full((1, 128), norm, jnp.float32)
    return lax.rsqrt(norm / entry_count + 1e-06), correlation / norm


def whole(value, like):
    return jnp.broadcast_to(value[:, :1], like.shape)


def first_kernel(entry_count, stats, *refs):
    images, outs = refs[:-2], refs[-2:]
    scale, _ = scale_theta(entry_count, stats)
    half = len(images) // 2
    for slot in range(2):
        at = 0
        for image in images[slot * half:(slot + 1) * half]:
            for step in range(image.shape[0]):
                value = image[step]
                outs[slot][:, at:at + value.shape[1]] = (value * whole(scale, value)).astype(jnp.bfloat16)
                at += value.shape[1]


def first_products(entry_count, stats, images):
    images = [image for row_images in images for image in row_images]
    tile = images[0].shape[1]
    width = sum(image.shape[0] for image in images) // 2 * tile
    return pl.pallas_call(
        functools.partial(first_kernel, entry_count),
        in_specs=[VMEM] * (1 + len(images)),
        out_specs=[VMEM] * 2,
        out_shape=[jax.ShapeDtypeStruct((tile, width), jnp.bfloat16)] * 2,
        cost_estimate=pl.CostEstimate(flops=4 * tile * width, bytes_accessed=12 * tile * width, transcendentals=0),
    )(stats, *images)


def second_value(entry_count, slot, local, first, step, left_sizes, right_sizes, stats, kept, arrived, image):
    tile = kept.shape[1]
    row, col = lax.axis_index("row") ^ slot, lax.axis_index("col")
    scale, theta = scale_theta(entry_count, stats)
    valid = valid_block((tile, tile), left_sizes, right_sizes, row, col * local + first + step)
    value = kept[step] + arrived[step].astype(jnp.float32)
    value = (value - whole(theta, value) * image[step]) * whole(scale, value)
    return jnp.where(valid, value, 0.0).astype(jnp.bfloat16)


def partner_kernel(entry_count, local, first, left_sizes, right_sizes, stats, kept, arrived, image, out):
    for step in range(kept.shape[0]):
        out[step] = second_value(
            entry_count, 1, local, first, step, left_sizes, right_sizes, stats, kept, arrived, image
        )


def partner_second(entry_count, local, first, left_sizes, right_sizes, stats, kept, arrived, image):
    return pl.pallas_call(
        functools.partial(partner_kernel, entry_count, local, first),
        in_specs=[SMEM, SMEM] + [VMEM] * 4,
        out_specs=VMEM,
        out_shape=jax.ShapeDtypeStruct(kept.shape, jnp.bfloat16),
        cost_estimate=pl.CostEstimate(flops=8 * kept.size, bytes_accessed=12 * kept.size, transcendentals=0),
    )(left_sizes, right_sizes, stats, kept, arrived, image)


def second_kernel(entry_count, left_sizes, right_sizes, stats, *refs):
    refs, out = refs[:-1], refs[-1]
    parts = len(refs) // 4
    kept, arrived, images, sent = (refs[i * parts:(i + 1) * parts] for i in range(4))
    local = sum(part.shape[0] for part in kept)
    tile = kept[0].shape[1]
    leading = leads(lax.axis_index("row")) == 1

    @pl.when(leading)
    def _():
        at = 0
        for part in range(parts):
            for step in range(kept[part].shape[0]):
                out[:, (at + step) * tile:(at + step + 1) * tile] = second_value(
                    entry_count, 0, local, at, step, left_sizes, right_sizes, stats, kept[part], arrived[part], images[part]
                )
            at += kept[part].shape[0]

    @pl.when(jnp.logical_not(leading))
    def _():
        at = 0
        for part in range(parts):
            for step in range(kept[part].shape[0]):
                out[:, (at + step) * tile:(at + step + 1) * tile] = sent[part][step]
            at += kept[part].shape[0]


def second_products(entry_count, left_sizes, right_sizes, stats, kept, arrived, images, sent):
    tile = kept[0].shape[1]
    width = sum(part.shape[0] for part in kept) * tile
    return pl.pallas_call(
        functools.partial(second_kernel, entry_count),
        in_specs=[SMEM, SMEM] + [VMEM] * (1 + 4 * len(kept)),
        out_specs=VMEM,
        out_shape=jax.ShapeDtypeStruct((tile, width), jnp.bfloat16),
        cost_estimate=pl.CostEstimate(flops=8 * tile * width, bytes_accessed=14 * tile * width, transcendentals=0),
    )(left_sizes, right_sizes, stats, *kept, *arrived, *images, *sent)


def on_device(wavefunction, left_ops, right_ops, left_dest, right_src, left_sizes, right_sizes):
    tile = left_ops.shape[2]
    local = right_ops.shape[1]
    row_count, col_count = lax.axis_size("row"), lax.axis_size("col")
    pair_bits, col_bits = bits_of(row_count) - 1, bits_of(col_count)
    entry_count = wavefunction.shape[0] * row_count * wavefunction.shape[1] * col_count
    both = ("row", "col")
    leading = leads(lax.axis_index("row")) == 1
    count = local // CHUNKS

    def gather(part):
        pieces = {0: part}
        for bit in reversed(range(col_bits)):
            for place in list(pieces):
                pieces[place | (1 << bit)] = lax.ppermute(pieces[place], "col", swap("col", 1 << bit))
        return [pieces[place] for place in range(col_count)]

    masked = pl.pallas_call(
        prepare_kernel,
        in_specs=[SMEM, SMEM, VMEM],
        out_specs=VMEM,
        out_shape=jax.ShapeDtypeStruct((local, tile, tile), wavefunction.dtype),
    )(left_sizes, right_sizes, wavefunction)
    left_own = left_ops[:, 0]
    masked_rows = [masked, lax.ppermute(masked, "row", swap("row", 1))]
    left = [left_own, lax.ppermute(left_own, "row", swap("row", 1))]

    def apply_h(pieces):
        out = []
        for first in range(0, local, count):
            sums = products(pieces, left, right_ops, right_src, left_dest, row_count, first, count)
            for bit in range(pair_bits):
                half = len(sums) // 2
                arrived = [lax.ppermute(part, both, leader_swap(1 << bit)) for part in sums[:half - 1:-1]][::-1]
                if bit < pair_bits - 1:
                    sums = [
                        (kept.astype(jnp.float32) + more.astype(jnp.float32)).astype(kept.dtype)
                        for kept, more in zip(sums[:half], arrived)
                    ]
            out.append((sums[:2], arrived))
        return out

    stats, images, image_pieces = 0.0, [[], []], [[[] for _ in range(col_count)] for _ in range(2)]
    for chunk, (kept, arrived) in enumerate(apply_h([gather(part) for part in masked_rows])):
        for slot in (1, 0):
            image, rounded, more = combine(
                slot, chunk * count, left_sizes, right_sizes, kept[slot], arrived[slot], masked_rows[slot]
            )
            stats = stats + more
            images[slot].append(image)
            for place, piece in enumerate(gather(rounded)):
                image_pieces[slot][place].append(piece)
    again = apply_h([[piece for place in places for piece in place] for places in image_pieces])
    for bit in range(col_bits):
        stats = stats + lax.ppermute(stats, "col", swap("col", 1 << bit))
    for bit in range(pair_bits):
        stats = stats + lax.ppermute(stats, both, leader_swap(1 << bit))
    firsts = first_products(entry_count, stats, images)
    first_product = jnp.where(leading, firsts[0], lax.ppermute(firsts[1], "row", swap("row", 1)))
    sent = [
        lax.ppermute(
            partner_second(
                entry_count, local, chunk * count, left_sizes, right_sizes, stats, kept[1], arrived[1], images[1][chunk]
            ),
            "row",
            swap("row", 1),
        )
        for chunk, (kept, arrived) in enumerate(again)
    ]
    second_product = second_products(
        entry_count, left_sizes, right_sizes, stats,
        [kept[0] for kept, _ in again], [arrived[0] for _, arrived in again], images[0], sent,
    )
    return (first_product, second_product)


def solution(mesh):
    placed = (
        P(("groups", "row"), "col"),
        P(None, ("groups", "row"), None, None),
        P(None, ("groups", "col"), None, None),
        P(None, "groups"),
        P(None, "groups"),
        P("groups"),
        P("groups"),
    )
    return jax.shard_map(
        on_device,
        mesh=mesh,
        in_specs=placed,
        out_specs=(P(("groups", "row"), "col"), P(("groups", "row"), "col")),
        check_vma=False,
    )
```

```python
import functools

import jax
import jax.numpy as jnp
from jax import lax
from jax.experimental import pallas as pl
from jax.experimental.pallas import tpu as pltpu
from jax.sharding import PartitionSpec as P

CHUNKS = 2
VMEM_LIMIT = 56 * 1024 * 1024
ANY = pl.BlockSpec(memory_space=pl.ANY)
SMEM = pl.BlockSpec(memory_space=pltpu.SMEM)


def bits_of(size):
    count = size.bit_length() - 1
    assert 1 << count == size
    return count


def swap(axis, bit):
    return [(place, place ^ bit) for place in range(lax.axis_size(axis))]


def leads(row):
    return (row ^ (row >> 1)) & 1


def leader_swap(bit):
    rows, cols = lax.axis_size("row"), lax.axis_size("col")
    pairs = []
    for row in range(rows):
        for col in range(cols):
            if leads(row):
                pair = (row >> 1) ^ bit
                there = (2 * pair if leads(2 * pair) else 2 * pair + 1, col)
            else:
                there = (row, col ^ 1)
            pairs.append((row * cols + col, there[0] * cols + there[1]))
    return pairs


def reverse_bits(value, count):
    out = 0
    for bit in range(count):
        out = out | (((value >> bit) & 1) << (count - 1 - bit))
    return out


def keep_corner(block, rows, cols):
    inside = (lax.broadcasted_iota(jnp.int32, block.shape, 0) < rows) & (
        lax.broadcasted_iota(jnp.int32, block.shape, 1) < cols
    )
    return jnp.where(inside, block.astype(jnp.float32), 0.0).astype(block.dtype)


def mask_left_kernel(left_dest, left_sizes, left, out):
    row = lax.axis_index("row")
    out[0] = keep_corner(left[0, 0], left_sizes[left_dest[pl.program_id(0), row]], left_sizes[row])


def mask_left(left_dest, left_sizes, left):
    terms, _, tile, _ = left.shape
    return pl.pallas_call(
        mask_left_kernel,
        grid=(terms,),
        in_specs=[SMEM, SMEM, pl.BlockSpec((1, 1, tile, tile), lambda term: (term, 0, 0, 0))],
        out_specs=pl.BlockSpec((1, tile, tile), lambda term: (term, 0, 0)),
        out_shape=jax.ShapeDtypeStruct((terms, tile, tile), left.dtype),
        compiler_params=pltpu.CompilerParams(vmem_limit_bytes=VMEM_LIMIT),
        cost_estimate=pl.CostEstimate(flops=left.size, bytes_accessed=4 * left.size, transcendentals=0),
    )(left_dest, left_sizes, left)


def mask_right_kernel(right_src, right_sizes, right, out):
    term, local = pl.program_id(0), right.shape[1]
    col = lax.axis_index("col")
    for place in range(local):
        block = col * local + place
        out[0, place] = keep_corner(right[0, place], right_sizes[block], right_sizes[right_src[term, block]])


def mask_right(right_src, right_sizes, right):
    terms, local, tile, _ = right.shape
    spec = pl.BlockSpec((1, local, tile, tile), lambda term: (term, 0, 0, 0))
    return pl.pallas_call(
        mask_right_kernel,
        grid=(terms,),
        in_specs=[SMEM, SMEM, spec],
        out_specs=spec,
        out_shape=jax.ShapeDtypeStruct(right.shape, right.dtype),
        compiler_params=pltpu.CompilerParams(vmem_limit_bytes=VMEM_LIMIT),
        cost_estimate=pl.CostEstimate(flops=right.size, bytes_accessed=4 * right.size, transcendentals=0),
    )(right_src, right_sizes, right)


def product_kernel(first, count, piece_count, row_count, source, target, *refs):
    pieces, refs = refs[:2 * piece_count], refs[2 * piece_count:]
    (left_own, left_near, left_far, right), refs = refs[:4], refs[4:]
    outs, (blocks, left, right_held, inner, total, kept, sent, in_sems, out_sems) = refs[:row_count], refs[row_count:]
    terms, local, tile = right.shape[:3]
    row, col = lax.axis_index("row"), lax.axis_index("col")
    started = []

    def start(here, there):
        copy = pltpu.make_async_copy(here, there, in_sems.at[len(started)])
        copy.start()
        started.append(copy)
        return copy

    right_copies = [start(right.at[:, first], right_held.at[0])]
    piece_copies = []
    for slot in range(2):
        at = 0
        for piece in pieces[slot * piece_count:(slot + 1) * piece_count]:
            for place in range(piece.shape[1] // tile):
                piece_copies.append(
                    start(piece.at[:, place * tile:(place + 1) * tile], blocks.at[at, slot * tile:(slot + 1) * tile])
                )
                at += 1
    half = terms // 2
    near = lax.rem(col, 2) * half
    left_copies = [
        start(left_own, left.at[0]),
        start(left_near, left.at[1, pl.ds(near, half)]),
        start(left_far, left.at[1, pl.ds(half - near, half)]),
    ]
    for step in range(1, count):
        right_copies.append(start(right.at[:, first + step], right_held.at[step]))

    out_copies = []
    for step in range(count):
        right_copies[step].wait()
        if step == 0:
            for copy in piece_copies:
                copy.wait()
        for term in range(terms):
            wanted = source[term, col * local + first + step]
            held = lax.bitwise_xor(lax.div(wanted, local), col) * local + lax.rem(wanted, local)
            inner[term] = lax.dot_general(
                blocks[held], right_held[step, term], (((1,), (1,)), ((), ())), preferred_element_type=jnp.float32
            ).astype(jnp.bfloat16)
        if step == 0:
            for copy in left_copies:
                copy.wait()
        total[...] = jnp.zeros_like(total)
        for term in range(terms):
            for slot in range(2):
                to = target[term, lax.bitwise_xor(row, slot)]
                to_slot = 2 * reverse_bits((to >> 1) ^ (row >> 1), bits_of(row_count) - 1) + 1 - leads(to)
                total[to_slot] += jnp.dot(
                    left[slot, term], inner[term, slot * tile:(slot + 1) * tile], preferred_element_type=jnp.float32
                )
        for slot in range(row_count):
            if slot < 2:
                held = kept.at[slot, step]
                held[...] = total[slot]
            else:
                held = sent.at[slot - 2, step]
                held[...] = total[slot].astype(sent.dtype)
            copy = pltpu.make_async_copy(
                held, outs[slot].at[:, step * tile:(step + 1) * tile], out_sems.at[len(out_copies)]
            )
            copy.start()
            out_copies.append(copy)
    for copy in out_copies:
        copy.wait()


def products(pieces, left, right, source, target, row_count, first, count):
    terms, local, tile = right.shape[:3]
    blocks = sum(piece.shape[1] for piece in pieces[0]) // tile
    pieces = [piece for row_pieces in pieces for piece in row_pieces]
    return pl.pallas_call(
        functools.partial(product_kernel, first, count, len(pieces) // 2, row_count),
        in_specs=[SMEM, SMEM] + [ANY] * (len(pieces) + 4),
        out_specs=[ANY] * row_count,
        out_shape=[
            jax.ShapeDtypeStruct((tile, count * tile), jnp.float32 if slot < 2 else jnp.bfloat16)
            for slot in range(row_count)
        ],
        scratch_shapes=[
            pltpu.VMEM((blocks, 2 * tile, tile), jnp.bfloat16),
            pltpu.VMEM((2, terms, tile, tile), jnp.bfloat16),
            pltpu.VMEM((count, terms, tile, tile), jnp.bfloat16),
            pltpu.VMEM((terms, 2 * tile, tile), jnp.bfloat16),
            pltpu.VMEM((row_count, tile, tile), jnp.float32),
            pltpu.VMEM((2, count, tile, tile), jnp.float32),
            pltpu.VMEM((row_count - 2, count, tile, tile), jnp.bfloat16),
            pltpu.SemaphoreType.DMA((count + 2 * blocks + 3,)),
            pltpu.SemaphoreType.DMA((count * row_count,)),
        ],
        compiler_params=pltpu.CompilerParams(vmem_limit_bytes=VMEM_LIMIT),
        cost_estimate=pl.CostEstimate(
            flops=8 * terms * count * tile**3,
            bytes_accessed=2 * tile * tile * (2 * blocks + terms * (2 + count) + count * (row_count + 2)),
            transcendentals=0,
        ),
    )(source, target, *pieces, *left, right)


def on_device(wavefunction, left_ops, right_ops, left_dest, right_src, left_sizes, right_sizes):
    tile = left_ops.shape[2]
    local = right_ops.shape[1]
    row_count, col_count = lax.axis_size("row"), lax.axis_size("col")
    pair_bits, col_bits = bits_of(row_count) - 1, bits_of(col_count)
    entry_count = wavefunction.shape[0] * row_count * wavefunction.shape[1] * col_count
    both = ("row", "col")
    row, col = lax.axis_index("row"), lax.axis_index("col")
    leading = leads(row) == 1
    count = local // CHUNKS
    width = count * tile

    def gather(part):
        pieces = {0: part}
        for bit in reversed(range(col_bits)):
            for place in list(pieces):
                pieces[place | (1 << bit)] = lax.ppermute(pieces[place], "col", swap("col", 1 << bit))
        return [pieces[place] for place in range(col_count)]

    vectors = [wavefunction, lax.ppermute(wavefunction, "row", swap("row", 1))]
    left_own = mask_left(left_dest, left_sizes, left_ops)
    half = left_ops.shape[0] // 2
    left_near = lax.dynamic_slice_in_dim(left_own, (col & 1) * half, half, 0)
    left_near = lax.ppermute(left_near, "row", swap("row", 1))
    left = [left_own, left_near, lax.ppermute(left_near, "col", swap("col", 1))]
    right = mask_right(right_src, right_sizes, right_ops)

    def apply_h(pieces):
        out = []
        for first in range(0, local, count):
            sums = products(pieces, left, right, right_src, left_dest, row_count, first, count)
            for bit in range(pair_bits):
                half = len(sums) // 2
                arrived = [lax.ppermute(part, both, leader_swap(1 << bit)) for part in sums[:half - 1:-1]][::-1]
                if bit < pair_bits - 1:
                    sums = [
                        (kept.astype(jnp.float32) + more.astype(jnp.float32)).astype(kept.dtype)
                        for kept, more in zip(sums[:half], arrived)
                    ]
            out.append((sums[:2], arrived))
        return out

    once = apply_h([gather(vector) for vector in vectors])
    pieces = [[[] for _ in range(col_count)] for _ in range(2)]
    for kept, arrived in once:
        for slot in (1, 0):
            rounded = (kept[slot] + arrived[slot].astype(jnp.float32)).astype(jnp.bfloat16)
            for place, piece in enumerate(gather(rounded)):
                pieces[slot][place].append(piece)
    again = apply_h([[piece for place in places for piece in place] for places in pieces])
    once, vectors, _ = lax.optimization_barrier((once, vectors, again[-1][0]))
    images = [
        [kept[slot] + arrived[slot].astype(jnp.float32) for kept, arrived in once] for slot in range(2)
    ]
    offsets = jnp.arange(tile)
    right_here = lax.dynamic_slice_in_dim(right_sizes, col * local, local, 0)
    col_valid = (offsets[None, :] < right_here[:, None]).reshape(-1)
    norm = correlation = 0.0
    for slot in range(2):
        row_valid = offsets < lax.dynamic_index_in_dim(left_sizes, row ^ slot, 0, keepdims=False)
        vector = jnp.where(row_valid[:, None] & col_valid[None, :], vectors[slot].astype(jnp.float32), 0.0)
        norm += jnp.sum(vector * vector)
        for chunk, image in enumerate(images[slot]):
            correlation += jnp.sum(vector[:, chunk * width:(chunk + 1) * width] * image)
    stats = jnp.broadcast_to(jnp.stack([norm, correlation])[:, None], (2, 128))
    for bit in range(col_bits):
        stats = stats + lax.ppermute(stats, "col", swap("col", 1 << bit))
    for bit in range(pair_bits):
        stats = stats + lax.ppermute(stats, both, leader_swap(1 << bit))
    norm, correlation = stats[0, 0], stats[1, 0]
    scale = lax.rsqrt(norm / entry_count + 1e-06)
    theta = correlation / norm

    def to_rows(of_slots):
        sent = [lax.ppermute(part, "row", swap("row", 1)) for part in of_slots[1]]
        return jnp.concatenate([jnp.where(leading, mine, theirs) for mine, theirs in zip(of_slots[0], sent)], 1)

    first_product = to_rows([[(image * scale).astype(jnp.bfloat16) for image in parts] for parts in images])
    second_product = to_rows([
        [
            ((kept[slot] - theta * image + arrived[slot].astype(jnp.float32)) * scale).astype(jnp.bfloat16)
            for (kept, arrived), image in zip(again, images[slot])
        ]
        for slot in range(2)
    ])
    return (first_product, second_product)


def solution(mesh):
    placed = (
        P(("groups", "row"), "col"),
        P(None, ("groups", "row"), None, None),
        P(None, ("groups", "col"), None, None),
        P(None, "groups"),
        P(None, "groups"),
        P("groups"),
        P("groups"),
    )
    return jax.shard_map(
        on_device,
        mesh=mesh,
        in_specs=placed,
        out_specs=(P(("groups", "row"), "col"), P(("groups", "row"), "col")),
        check_vma=False,
    )
```

```python
import functools

import jax
import jax.numpy as jnp
from jax import lax
from jax.experimental import pallas as pl
from jax.experimental.pallas import tpu as pltpu
from jax.sharding import PartitionSpec as P

MIB = 1024 * 1024
CODE_ROWS = 16
VMEM_LIMIT = 10 * MIB
MASK_LIMIT = 60 * MIB
ANY = pl.BlockSpec(memory_space=pl.ANY)
BRIEF = pl.CostEstimate(flops=10**9, bytes_accessed=0, transcendentals=0)
TOKEN = jax.ShapeDtypeStruct((2, 8, 128), jnp.float32)
VMEM = pl.BlockSpec(memory_space=pltpu.VMEM)
SMEM = pl.BlockSpec(memory_space=pltpu.SMEM)


def bits_of(size):
    count = size.bit_length() - 1
    assert 1 << count == size
    return count


def swap(axis, bit):
    return [(place, place ^ bit) for place in range(lax.axis_size(axis))]


def leads(row):
    return (row ^ (row >> 1)) & 1


def leader_swap(bit):
    rows, cols = lax.axis_size("row"), lax.axis_size("col")
    pairs = []
    for row in range(rows):
        for col in range(cols):
            if leads(row):
                pair = (row >> 1) ^ bit
                there = (2 * pair if leads(2 * pair) else 2 * pair + 1, col)
            else:
                there = (row, col ^ 1)
            pairs.append((row * cols + col, there[0] * cols + there[1]))
    return pairs


def reverse_bits(value, count):
    out = 0
    for bit in range(count):
        out = out | (((value >> bit) & 1) << (count - 1 - bit))
    return out


def keep_corner(block, rows, cols):
    inside = (lax.broadcasted_iota(jnp.int32, block.shape, 0) < rows) & (
        lax.broadcasted_iota(jnp.int32, block.shape, 1) < cols
    )
    return jnp.where(inside, block.astype(jnp.float32), 0.0).astype(block.dtype)


def mask_left_kernel(left_dest, left_sizes, left, out, near):
    row, col = lax.axis_index("row"), lax.axis_index("col")
    terms, half = out.shape[0], near.shape[0]
    for term in range(terms):
        out[term] = keep_corner(left[term, 0], left_sizes[left_dest[term, row]], left_sizes[row])
    for place in range(half):
        near[place] = out[lax.rem(col, 2) * half + place]


def mask_left(left_dest, left_sizes, left):
    terms, _, tile, _ = left.shape
    return pl.pallas_call(
        mask_left_kernel,
        in_specs=[SMEM, SMEM, VMEM],
        out_specs=[VMEM, VMEM],
        out_shape=[jax.ShapeDtypeStruct((count, tile, tile), left.dtype) for count in (terms, terms // 2)],
        compiler_params=pltpu.CompilerParams(vmem_limit_bytes=MASK_LIMIT),
        cost_estimate=BRIEF,
    )(left_dest, left_sizes, left)


def mask_right_kernel(right_src, right_sizes, right, *outs):
    col = lax.axis_index("col")
    for step in range(right.shape[0]):
        term = pl.program_id(0) * right.shape[0] + step
        for place, out in enumerate(outs):
            block = col * len(outs) + place
            out[step] = keep_corner(right[step, place], right_sizes[block], right_sizes[right_src[term, block]])


def mask_right(right_src, right_sizes, right):
    terms, local, tile, _ = right.shape
    return pl.pallas_call(
        mask_right_kernel,
        grid=(terms // 2,),
        in_specs=[SMEM, SMEM, pl.BlockSpec((2, local, tile, tile), lambda step: (step, 0, 0, 0))],
        out_specs=[pl.BlockSpec((2, tile, tile), lambda step: (step, 0, 0))] * local,
        out_shape=[jax.ShapeDtypeStruct((terms, tile, tile), right.dtype)] * local,
        compiler_params=pltpu.CompilerParams(vmem_limit_bytes=MASK_LIMIT),
        cost_estimate=BRIEF,
    )(right_src, right_sizes, right)


def place_kernel(places, *refs):
    pieces, (blocks, sems) = refs[:len(places)], refs[-2:]
    tile = blocks.shape[2]
    copies = []

    def add(here, there):
        copies.append(pltpu.make_async_copy(here, there, sems.at[len(copies)]))

    for (block, slot), piece in zip(places, pieces):
        if len(piece.shape) == 3:
            add(piece.at[:, :blocks.shape[1]], blocks.at[block:block + piece.shape[0]])
        else:
            for at in range(piece.shape[1] // tile):
                rows = piece.shape[0]
                add(piece.at[:, at * tile:(at + 1) * tile], blocks.at[block + at, slot * tile:slot * tile + rows])
    for copy in copies:
        copy.start()
    for copy in copies:
        copy.wait()


def place(blocks, shape, pieces, tokens=()):
    places, pieces = [at for at, _ in pieces], [piece for _, piece in pieces]
    copies = sum(1 if piece.ndim == 3 else piece.shape[1] // shape[2] for piece in pieces)
    rest = list(tokens) if blocks is None else [blocks, *tokens]
    return pl.pallas_call(
        functools.partial(place_kernel, places),
        in_specs=[ANY] * (len(pieces) + len(rest)),
        out_specs=ANY,
        out_shape=jax.ShapeDtypeStruct(shape, jnp.bfloat16),
        scratch_shapes=[pltpu.SemaphoreType.DMA((copies,))],
        input_output_aliases={} if blocks is None else {len(pieces): 0},
        compiler_params=pltpu.CompilerParams(vmem_limit_bytes=VMEM_LIMIT),
        cost_estimate=BRIEF,
    )(*pieces, *rest)


def join_kernel(*refs):
    held, pieces = refs[-1], refs[:refs[-1].shape[0]]
    rows = held.shape[1] - CODE_ROWS
    sums = [jnp.zeros((1, 1), jnp.float32)] * 2
    for at, piece in enumerate(pieces):
        held[at, :rows] = piece[:rows]
        sums = [total + more for total, more in zip(sums, decode(piece[rows:]))]
        if at:
            held[at, rows:] = jnp.zeros((CODE_ROWS, held.shape[2]), held.dtype)
    held[0, rows:] = encode(sums)


def join(pieces, tokens):
    return pl.pallas_call(
        join_kernel,
        in_specs=[VMEM] * len(pieces) + [ANY] * len(tokens),
        out_specs=VMEM,
        out_shape=jax.ShapeDtypeStruct((len(pieces), *pieces[0].shape), pieces[0].dtype),
        compiler_params=pltpu.CompilerParams(vmem_limit_bytes=VMEM_LIMIT),
        cost_estimate=BRIEF,
    )(*pieces, *tokens)


def read_codes(arrays, codes, sems):
    copies = [
        pltpu.make_async_copy(ref.at[0, ref.shape[1] - CODE_ROWS:], codes.at[at], sems.at[at])
        for at, ref in enumerate(arrays)
    ]
    for copy in copies:
        copy.start()
    for copy in copies:
        copy.wait()
    return jnp.stack([jnp.broadcast_to(sum(pair), (8, 128)) for pair in zip(decode(codes[0]), decode(codes[1]))])


def settle_kernel(held, arrived, *refs):
    out, codes, sems = refs[-3:]
    out[...] = read_codes((held, arrived), codes, sems)


def settle(held, arrived, tokens):
    return pl.pallas_call(
        settle_kernel,
        in_specs=[ANY] * (2 + len(tokens)),
        out_specs=VMEM,
        out_shape=jax.ShapeDtypeStruct((2, 8, 128), jnp.float32),
        scratch_shapes=[pltpu.VMEM((2, CODE_ROWS, held.shape[2]), held.dtype), pltpu.SemaphoreType.DMA((2,))],
        compiler_params=pltpu.CompilerParams(vmem_limit_bytes=VMEM_LIMIT),
        cost_estimate=BRIEF,
    )(held, arrived, *tokens)


def product_kernel(first, local, out_slots, coded, source, target, blocks, left_own, left_near, left_far, right, *refs):
    outs, (token, inner, total, held_right, sem, codes, code_sems) = refs[-7 - len(out_slots):-7], refs[-7:]
    pair_count = total.shape[0] // 2
    if coded:
        token[...] = read_codes(refs[:2], codes, code_sems)
    else:
        token[...] = jnp.zeros_like(token)
    copy = pltpu.make_async_copy(right, held_right, sem)
    copy.start()
    total[...] = jnp.zeros_like(total)
    copy.wait()
    terms, tile = right.shape[:2]
    row, col = lax.axis_index("row"), lax.axis_index("col")
    for term in range(terms):
        wanted = source[term, col * local + first]
        place_of = lax.bitwise_xor(lax.div(wanted, local), col)
        place_of = (place_of >> 1) + (place_of & 1) * (blocks.shape[0] // local // 2)
        held = place_of * local + lax.rem(wanted, local)
        inner[term] = lax.dot_general(
            blocks[held], held_right[term], (((1,), (1,)), ((), ())), preferred_element_type=jnp.float32
        ).astype(jnp.bfloat16)

    def add(left, term, slot):
        to = target[term, lax.bitwise_xor(row, slot)]
        to_slot = 2 * reverse_bits((to >> 1) ^ (row >> 1), bits_of(pair_count)) + 1 - leads(to)
        total[to_slot] += jnp.dot(left, inner[term, slot * tile:(slot + 1) * tile], preferred_element_type=jnp.float32)

    half = terms // 2
    near = lax.rem(col, 2) * half
    for term in range(terms):
        add(left_own[term], term, 0)
    for step in range(half):
        add(left_near[step], near + step, 1)
        add(left_far[step], half - near + step, 1)
    for slots, out in zip(out_slots, outs):
        for at, slot in enumerate(slots):
            out[at * tile:(at + 1) * tile] = total[slot].astype(out.dtype)
        if coded and slots[0] >= 2:
            out[len(slots) * tile:] = encode([token[0, :1, :1], token[1, :1, :1]])


def products(blocks, left, right, source, target, out_slots, first, tokens, coded=()):
    local, (terms, tile) = len(right), right[0].shape[:2]
    out_shape = [
        jax.ShapeDtypeStruct((len(slots) * tile + CODE_ROWS, tile), jnp.bfloat16)
        if coded and slots[0] >= 2
        else jax.ShapeDtypeStruct((len(slots) * tile, tile), jnp.bfloat16 if slots[0] >= 2 else jnp.float32)
        for slots in out_slots
    ] + [TOKEN]
    held = 2 * blocks.size + 8 * terms * tile * tile + sum(8 * out.size for out in out_shape)
    return pl.pallas_call(
        functools.partial(product_kernel, first, local, out_slots, bool(coded)),
        in_specs=[SMEM, SMEM] + [VMEM] * 4 + [ANY] * (1 + len(coded) + len(tokens)),
        out_specs=[VMEM] * (len(out_slots) + 1),
        out_shape=out_shape,
        scratch_shapes=[
            pltpu.VMEM((terms, 2 * tile, tile), jnp.bfloat16),
            pltpu.VMEM((sum(len(slots) for slots in out_slots), tile, tile), jnp.float32),
            pltpu.VMEM((terms, tile, tile), jnp.bfloat16),
            pltpu.SemaphoreType.DMA,
            pltpu.VMEM((2, CODE_ROWS, tile), jnp.bfloat16),
            pltpu.SemaphoreType.DMA((2,)),
        ],
        compiler_params=pltpu.CompilerParams(vmem_limit_bytes=held + 4 * MIB),
        cost_estimate=BRIEF,
    )(source, target, blocks, *left, right[first], *coded, *tokens)


def encode(values):
    rows = lax.broadcasted_iota(jnp.int32, (CODE_ROWS, 256), 0)
    out = jnp.zeros((CODE_ROWS, 256), jnp.float32)
    for at, value in enumerate(values):
        rest = jnp.broadcast_to(value, out.shape)
        for part in range(3):
            head = rest.astype(jnp.bfloat16).astype(jnp.float32)
            out = jnp.where(rows == 3 * at + part, head, out)
            rest = rest - head
    return out.astype(jnp.bfloat16)


def decode(code):
    code = code[:6, :1].astype(jnp.float32)
    return [code[at:at + 1] + code[at + 1:at + 2] + code[at + 2:at + 3] for at in (0, 3)]


def combine_kernel(first, local, left_sizes, right_sizes, kept, arrived, blocks, *refs):
    before = refs[0]
    both, near, stats, held, sem = refs[-5:]
    tile = near.shape[0]
    copy = pltpu.make_async_copy(blocks.at[first], held, sem)
    copy.start()
    row, col = lax.axis_index("row"), lax.axis_index("col")
    image = kept[...] + arrived[...].astype(jnp.float32)
    both[:2 * tile] = image.astype(both.dtype)
    near[...] = image[tile:].astype(near.dtype)
    copy.wait()
    norm = correlation = jnp.zeros((8, tile), jnp.float32)
    for slot in range(2):
        rows = pl.ds(slot * tile, tile)
        masked = keep_corner(held[rows], left_sizes[lax.bitwise_xor(row, slot)], right_sizes[col * local + first])
        masked = masked.astype(jnp.float32)
        norm += jnp.sum((masked * masked).reshape(-1, 8, tile), 0)
        correlation += jnp.sum((masked * image[slot * tile:(slot + 1) * tile]).reshape(-1, 8, tile), 0)
    if first:
        norm, correlation = norm + before[0], correlation + before[1]
    stats[0] = norm
    stats[1] = correlation
    if first == local - 1:
        both[2 * tile:] = encode([jnp.sum(norm), jnp.sum(correlation)])


def combine(first, local, left_sizes, right_sizes, kept, arrived, blocks, stats, tokens):
    tile = kept.shape[1]
    rows = 2 * tile + CODE_ROWS * (first == local - 1)
    more = ([stats] if first else []) + tokens
    return pl.pallas_call(
        functools.partial(combine_kernel, first, local),
        in_specs=[SMEM, SMEM, VMEM, VMEM, ANY] + ([VMEM] if first else []) + [ANY] * len(tokens),
        out_specs=[VMEM] * 3,
        out_shape=[jax.ShapeDtypeStruct((height, tile), arrived.dtype) for height in (rows, tile)]
        + [jax.ShapeDtypeStruct((2, 8, tile), jnp.float32)],
        scratch_shapes=[pltpu.VMEM((2 * tile, tile), blocks.dtype), pltpu.SemaphoreType.DMA],
        compiler_params=pltpu.CompilerParams(vmem_limit_bytes=VMEM_LIMIT),
        cost_estimate=BRIEF,
    )(left_sizes, right_sizes, kept, arrived, blocks, *more)


def emit_kernel(start, coded, kept, arrived, *refs):
    outs = refs[-1 - coded:]
    tile = kept.shape[1]
    outs[0][:tile] = (kept[tile:] + arrived[start:start + tile].astype(jnp.float32)).astype(outs[0].dtype)
    if coded:
        more = decode(arrived[arrived.shape[0] - CODE_ROWS:])
        stats = [refs[0][at, :1, :1] + more[at] for at in range(2)]
        outs[0][tile:] = encode(stats)
        for at, value in enumerate(stats):
            outs[1][at] = jnp.broadcast_to(value, outs[1].shape[1:])


def emit(kept, arrived, tokens, stats=None):
    tile, coded = kept.shape[1], stats is not None
    start = tile if arrived.shape[0] >= 2 * tile else 0
    return pl.pallas_call(
        functools.partial(emit_kernel, start, coded),
        in_specs=[VMEM] * (2 + coded) + [ANY] * len(tokens),
        out_specs=[VMEM] * (1 + coded),
        out_shape=[jax.ShapeDtypeStruct((tile + CODE_ROWS * coded, tile), arrived.dtype)] + [TOKEN] * coded,
        compiler_params=pltpu.CompilerParams(vmem_limit_bytes=VMEM_LIMIT),
        cost_estimate=BRIEF,
    )(kept, arrived, *([stats] if coded else []), *tokens)


def scales_kernel(entry_count, own, sent, out, code, sem):
    copy = pltpu.make_async_copy(sent.at[sent.shape[0] - CODE_ROWS:], code, sem)
    copy.start()
    copy.wait()
    leading = leads(lax.axis_index("row")) == 1
    norm, correlation = (
        jnp.where(leading, mine, jnp.broadcast_to(theirs, mine.shape))
        for mine, theirs in zip((own[0], own[1]), decode(code[...]))
    )
    out[0] = lax.rsqrt(norm / entry_count + 1e-06)
    out[1] = correlation / norm


def scales(entry_count, own, sent):
    return pl.pallas_call(
        functools.partial(scales_kernel, entry_count),
        in_specs=[VMEM, ANY],
        out_specs=VMEM,
        out_shape=TOKEN,
        scratch_shapes=[pltpu.VMEM((CODE_ROWS, sent.shape[1]), sent.dtype), pltpu.SemaphoreType.DMA],
        compiler_params=pltpu.CompilerParams(vmem_limit_bytes=VMEM_LIMIT),
        cost_estimate=BRIEF,
    )(own, sent)


def after(value, *others):
    return pl.pallas_call(
        lambda *refs: None,
        in_specs=[ANY] * (1 + len(others)),
        out_specs=ANY,
        out_shape=jax.ShapeDtypeStruct(value.shape, value.dtype),
        input_output_aliases={0: 0},
        cost_estimate=BRIEF,
    )(value, *others)


def on_device(wavefunction, left_ops, right_ops, left_dest, right_src, left_sizes, right_sizes):
    tile = left_ops.shape[2]
    local = right_ops.shape[1]
    row_count, col_count = lax.axis_size("row"), lax.axis_size("col")
    pair_bits, col_bits = bits_of(row_count) - 1, bits_of(col_count)
    entry_count = wavefunction.shape[0] * row_count * wavefunction.shape[1] * col_count
    both = ("row", "col")
    row, col = lax.axis_index("row"), lax.axis_index("col")
    leading = leads(row) == 1
    blocks_shape = (col_count * local, 2 * tile, tile)

    def far(part):
        pieces = [part]
        for bit in range(1, col_bits):
            pieces += [lax.ppermute(piece, "col", swap("col", 1 << bit)) for piece in pieces]
        return pieces

    def other_core(part):
        return lax.ppermute(part, "col", swap("col", 1))

    def block_of(piece, odd):
        return (odd * (col_count // 2) + piece) * local

    def to_partner(part):
        return lax.ppermute(part, "row", swap("row", 1))

    near = to_partner(wavefunction)
    left_own, left_near = mask_left(left_dest, left_sizes, left_ops)
    left_near = to_partner(left_near)
    left = [left_own, left_near, other_core(left_near)]
    right = mask_right(right_src, right_sizes, right_ops)
    near = after(near, left_own, right[0])

    def exchange(sums):
        kept, sums = sums[0], sums[1:]
        per_pair = len(sums) // ((1 << pair_bits) - 1)
        for bit in range(pair_bits):
            half = (len(sums) + per_pair) // 2 - per_pair
            arrived = [lax.ppermute(part, both, leader_swap(1 << bit)) for part in sums[half:][::-1]][::-1]
            if bit < pair_bits - 1:
                mine = arrived[0] if per_pair == 1 else jnp.concatenate(arrived[:per_pair], 0)
                kept = kept + mine.astype(jnp.float32)
                sums = [
                    (part.astype(jnp.float32) + more.astype(jnp.float32)).astype(part.dtype)
                    for part, more in zip(sums[:half], arrived[per_pair:])
                ]
        return kept, arrived

    joined = [(2 * pair, 2 * pair + 1) for pair in range(1 << pair_bits)]
    apart = joined[:1] + [(slot,) for pair in joined[1:] for slot in pair]

    def multiply(blocks, slots, first, tokens, coded=()):
        return products(blocks, left, right, right_src, left_dest, slots, first, tokens, coded)

    pieces = [((block_of(at, 0), 0), piece) for at, piece in enumerate(far(wavefunction))]
    near_pieces = [((block_of(at, 0), 1), piece) for at, piece in enumerate(far(near))]
    blocks = None
    for several in (pieces + near_pieces[:1], near_pieces[1:]):
        blocks = place(blocks, blocks_shape, several + [
            ((block + block_of(0, 1), slot), other_core(piece)) for (block, slot), piece in several
        ])

    once, parts, near_images, stats, token = [], [], [], None, None
    for first in range(local + 1):
        if first < local:
            *sums, token = multiply(blocks, joined, first, ([token] if first else []) + ([stats] if parts else []))
            once.append(exchange(sums))
        for done in range(len(parts), first if first < local else local):
            kept, (arrived,) = once[done]
            image, near_image, stats = combine(
                done, local, left_sizes, right_sizes, kept, arrived, blocks, stats,
                [token] + (parts[0][1:] if done > 1 else []),
            )
            parts.append(far(image))
            near_images.append(to_partner(near_image))
    blocks = None
    for group in (range(local - 1), range(local - 1, local)):
        if blocks is None:
            held = place(
                None,
                (len(group) * col_count // 2, 2 * tile, tile),
                [((at * len(group) + i, 0), parts[first][at]) for at in range(col_count // 2) for i, first in enumerate(group)],
                [parts[-1][0], *near_images[:-2]],
            )
        else:
            held = join(parts[-1], [blocks, *near_images[-2:]])
        arrived_held = other_core(held)
        blocks = place(blocks, blocks_shape, [
            ((block_of(at, odd) + group[0], 0), half[at * len(group):(at + 1) * len(group)])
            for odd, half in enumerate((held, arrived_held))
            for at in range(col_count // 2)
        ])

    carrier = local - 2 if pair_bits == 1 else local
    again, near_again, token, stats = [], [], None, None
    for first in range(local + 1):
        if first < local:
            slots = apart if first == local - 1 else joined
            tokens = ([token] if first else []) + ([near_again[-1]] if near_again else [])
            coded = [held, arrived_held] if first == carrier else []
            *sums, token = multiply(blocks, slots, first, tokens, coded)
            stats = token if coded else stats
            again.append(exchange(sums))
        for done in range(len(near_again), first if first < local else local):
            kept, arrived = again[done]
            tokens = [token]
            if done == carrier:
                near, stats = emit(kept, arrived[-1], tokens, stats)
            else:
                (near,) = emit(kept, arrived[-1], tokens)
            near_again.append(near)
    near_again = [to_partner(part) for part in near_again]
    if carrier < local:
        both_scales = scales(entry_count, stats, near_again[carrier])
        scale, theta = both_scales[0, 0, 0], both_scales[1, 0, 0]
    else:
        stats = settle(held, arrived_held, [token])
        for bit in range(pair_bits):
            stats = stats + lax.ppermute(stats, both, leader_swap(1 << bit))
        stats = jnp.where(leading, stats, to_partner(stats))
        norm, correlation = stats[0, 0, 0], stats[1, 0, 0]
        scale = lax.rsqrt(norm / entry_count + 1e-06)
        theta = correlation / norm

    images = [
        jnp.where(leading, part[0][:tile], near_image).astype(jnp.float32) for part, near_image in zip(parts, near_images)
    ]
    again = [
        jnp.where(leading, kept[:tile] + arrived[0][:tile].astype(jnp.float32), near[:tile].astype(jnp.float32))
        for (kept, arrived), near in zip(again, near_again)
    ]
    first_product = jnp.concatenate([(image * scale).astype(jnp.bfloat16) for image in images], 1)
    second_product = jnp.concatenate(
        [((more - theta * image) * scale).astype(jnp.bfloat16) for more, image in zip(again, images)], 1
    )
    return (first_product, second_product)


def solution(mesh):
    placed = (
        P(("groups", "row"), "col"),
        P(None, ("groups", "row"), None, None),
        P(None, ("groups", "col"), None, None),
        P(None, "groups"),
        P(None, "groups"),
        P("groups"),
        P("groups"),
    )
    return jax.shard_map(
        on_device,
        mesh=mesh,
        in_specs=placed,
        out_specs=(P(("groups", "row"), "col"), P(("groups", "row"), "col")),
        check_vma=False,
    )
```

```python
import functools

import jax
import jax.numpy as jnp
from jax import lax
from jax.experimental import pallas as pl
from jax.experimental.pallas import tpu as pltpu
from jax.sharding import PartitionSpec as P

MIB = 1024 * 1024
CODE_ROWS = 16
VMEM_LIMIT = 10 * MIB
MASK_LIMIT = 60 * MIB
ANY = pl.BlockSpec(memory_space=pl.ANY)
BRIEF = pl.CostEstimate(flops=10**9, bytes_accessed=0, transcendentals=0)
TOKEN = jax.ShapeDtypeStruct((2, 8, 128), jnp.float32)
VMEM = pl.BlockSpec(memory_space=pltpu.VMEM)
SMEM = pl.BlockSpec(memory_space=pltpu.SMEM)


def bits_of(size):
    count = size.bit_length() - 1
    assert 1 << count == size
    return count


def swap(axis, bit):
    return [(place, place ^ bit) for place in range(lax.axis_size(axis))]


def leads(row):
    return (row ^ (row >> 1)) & 1


def leader_swap(bit):
    rows, cols = lax.axis_size("row"), lax.axis_size("col")
    pairs = []
    for row in range(rows):
        for col in range(cols):
            if leads(row):
                pair = (row >> 1) ^ bit
                there = (2 * pair if leads(2 * pair) else 2 * pair + 1, col)
            else:
                there = (row, col ^ 1)
            pairs.append((row * cols + col, there[0] * cols + there[1]))
    return pairs


def reverse_bits(value, count):
    out = 0
    for bit in range(count):
        out = out | (((value >> bit) & 1) << (count - 1 - bit))
    return out


def keep_corner(block, rows, cols):
    inside = (lax.broadcasted_iota(jnp.int32, block.shape, 0) < rows) & (
        lax.broadcasted_iota(jnp.int32, block.shape, 1) < cols
    )
    return jnp.where(inside, block.astype(jnp.float32), 0.0).astype(block.dtype)


def mask_left_kernel(left_dest, left_sizes, left, out, near):
    row, col = lax.axis_index("row"), lax.axis_index("col")
    terms, half = out.shape[0], near.shape[0]
    for term in range(terms):
        out[term] = keep_corner(left[term, 0], left_sizes[left_dest[term, row]], left_sizes[row])
    for place in range(half):
        near[place] = out[lax.rem(col, 2) * half + place]


def mask_left(left_dest, left_sizes, left):
    terms, _, tile, _ = left.shape
    return pl.pallas_call(
        mask_left_kernel,
        in_specs=[SMEM, SMEM, VMEM],
        out_specs=[VMEM, VMEM],
        out_shape=[jax.ShapeDtypeStruct((count, tile, tile), left.dtype) for count in (terms, terms // 2)],
        compiler_params=pltpu.CompilerParams(vmem_limit_bytes=MASK_LIMIT),
        cost_estimate=BRIEF,
    )(left_dest, left_sizes, left)


def mask_right_kernel(right_src, right_sizes, right, *outs):
    col = lax.axis_index("col")
    for step in range(right.shape[0]):
        term = pl.program_id(0) * right.shape[0] + step
        for place, out in enumerate(outs):
            block = col * len(outs) + place
            out[step] = keep_corner(right[step, place], right_sizes[block], right_sizes[right_src[term, block]])


def mask_right(right_src, right_sizes, right):
    terms, local, tile, _ = right.shape
    return pl.pallas_call(
        mask_right_kernel,
        grid=(terms // 2,),
        in_specs=[SMEM, SMEM, pl.BlockSpec((2, local, tile, tile), lambda step: (step, 0, 0, 0))],
        out_specs=[pl.BlockSpec((2, tile, tile), lambda step: (step, 0, 0))] * local,
        out_shape=[jax.ShapeDtypeStruct((terms, tile, tile), right.dtype)] * local,
        compiler_params=pltpu.CompilerParams(vmem_limit_bytes=MASK_LIMIT),
        cost_estimate=BRIEF,
    )(right_src, right_sizes, right)


def place_kernel(places, *refs):
    pieces, (blocks, sems) = refs[:len(places)], refs[-2:]
    tile = blocks.shape[2]
    copies = []

    def add(here, there):
        copies.append(pltpu.make_async_copy(here, there, sems.at[len(copies)]))

    for (block, slot), piece in zip(places, pieces):
        if len(piece.shape) == 3:
            add(piece.at[:, :blocks.shape[1]], blocks.at[block:block + piece.shape[0]])
        else:
            for at in range(piece.shape[1] // tile):
                rows = piece.shape[0]
                add(piece.at[:, at * tile:(at + 1) * tile], blocks.at[block + at, slot * tile:slot * tile + rows])
    for copy in copies:
        copy.start()
    for copy in copies:
        copy.wait()


def place(blocks, shape, pieces, tokens=()):
    places, pieces = [at for at, _ in pieces], [piece for _, piece in pieces]
    copies = sum(1 if piece.ndim == 3 else piece.shape[1] // shape[2] for piece in pieces)
    rest = list(tokens) if blocks is None else [blocks, *tokens]
    return pl.pallas_call(
        functools.partial(place_kernel, places),
        in_specs=[ANY] * (len(pieces) + len(rest)),
        out_specs=ANY,
        out_shape=jax.ShapeDtypeStruct(shape, jnp.bfloat16),
        scratch_shapes=[pltpu.SemaphoreType.DMA((copies,))],
        input_output_aliases={} if blocks is None else {len(pieces): 0},
        compiler_params=pltpu.CompilerParams(vmem_limit_bytes=VMEM_LIMIT),
        cost_estimate=BRIEF,
    )(*pieces, *rest)


def join_kernel(*refs):
    held, pieces = refs[-1], refs[:refs[-1].shape[0]]
    rows = held.shape[1] - CODE_ROWS
    sums = [jnp.zeros((1, 1), jnp.float32)] * 2
    for at, piece in enumerate(pieces):
        held[at, :rows] = piece[:rows]
        sums = [total + more for total, more in zip(sums, decode(piece[rows:]))]
        if at:
            held[at, rows:] = jnp.zeros((CODE_ROWS, held.shape[2]), held.dtype)
    held[0, rows:] = encode(sums)


def join(pieces, tokens):
    return pl.pallas_call(
        join_kernel,
        in_specs=[VMEM] * len(pieces) + [ANY] * len(tokens),
        out_specs=VMEM,
        out_shape=jax.ShapeDtypeStruct((len(pieces), *pieces[0].shape), pieces[0].dtype),
        compiler_params=pltpu.CompilerParams(vmem_limit_bytes=VMEM_LIMIT),
        cost_estimate=BRIEF,
    )(*pieces, *tokens)


def read_codes(arrays, codes, sems):
    copies = [
        pltpu.make_async_copy(ref.at[0, ref.shape[1] - CODE_ROWS:], codes.at[at], sems.at[at])
        for at, ref in enumerate(arrays)
    ]
    for copy in copies:
        copy.start()
    for copy in copies:
        copy.wait()
    return jnp.stack([jnp.broadcast_to(sum(pair), (8, 128)) for pair in zip(decode(codes[0]), decode(codes[1]))])


def settle_kernel(held, arrived, *refs):
    out, codes, sems = refs[-3:]
    out[...] = read_codes((held, arrived), codes, sems)


def settle(held, arrived, tokens):
    return pl.pallas_call(
        settle_kernel,
        in_specs=[ANY] * (2 + len(tokens)),
        out_specs=VMEM,
        out_shape=jax.ShapeDtypeStruct((2, 8, 128), jnp.float32),
        scratch_shapes=[pltpu.VMEM((2, CODE_ROWS, held.shape[2]), held.dtype), pltpu.SemaphoreType.DMA((2,))],
        compiler_params=pltpu.CompilerParams(vmem_limit_bytes=VMEM_LIMIT),
        cost_estimate=BRIEF,
    )(held, arrived, *tokens)


def product_kernel(first, local, out_slots, coded, source, target, blocks, left_own, left_near, left_far, right, *refs):
    outs, (token, inner, total, held_right, sem, codes, code_sems) = refs[-7 - len(out_slots):-7], refs[-7:]
    pair_count = total.shape[0] // 2
    if coded:
        token[...] = read_codes(refs[:2], codes, code_sems)
    else:
        token[...] = jnp.zeros_like(token)
    copy = pltpu.make_async_copy(right, held_right, sem)
    copy.start()
    total[...] = jnp.zeros_like(total)
    copy.wait()
    terms, tile = right.shape[:2]
    row, col = lax.axis_index("row"), lax.axis_index("col")
    for term in range(terms):
        wanted = source[term, col * local + first]
        place_of = lax.bitwise_xor(lax.div(wanted, local), col)
        place_of = (place_of >> 1) + (place_of & 1) * (blocks.shape[0] // local // 2)
        held = place_of * local + lax.rem(wanted, local)
        inner[term] = lax.dot_general(
            blocks[held], held_right[term], (((1,), (1,)), ((), ())), preferred_element_type=jnp.float32
        ).astype(jnp.bfloat16)

    def add(left, term, slot):
        to = target[term, lax.bitwise_xor(row, slot)]
        to_slot = 2 * reverse_bits((to >> 1) ^ (row >> 1), bits_of(pair_count)) + 1 - leads(to)
        total[to_slot] += jnp.dot(left, inner[term, slot * tile:(slot + 1) * tile], preferred_element_type=jnp.float32)

    half = terms // 2
    near = lax.rem(col, 2) * half
    for term in range(terms):
        add(left_own[term], term, 0)
    for step in range(half):
        add(left_near[step], near + step, 1)
        add(left_far[step], half - near + step, 1)
    for slots, out in zip(out_slots, outs):
        for at, slot in enumerate(slots):
            out[at * tile:(at + 1) * tile] = total[slot].astype(out.dtype)
        if coded and slots[0] >= 2:
            out[len(slots) * tile:] = encode([token[0, :1, :1], token[1, :1, :1]])


def products(blocks, left, right, source, target, out_slots, first, tokens, coded=()):
    local, (terms, tile) = len(right), right[0].shape[:2]
    out_shape = [
        jax.ShapeDtypeStruct((len(slots) * tile + CODE_ROWS, tile), jnp.bfloat16)
        if coded and slots[0] >= 2
        else jax.ShapeDtypeStruct((len(slots) * tile, tile), jnp.bfloat16 if slots[0] >= 2 else jnp.float32)
        for slots in out_slots
    ] + [TOKEN]
    held = 2 * blocks.size + 8 * terms * tile * tile + sum(8 * out.size for out in out_shape)
    return pl.pallas_call(
        functools.partial(product_kernel, first, local, out_slots, bool(coded)),
        in_specs=[SMEM, SMEM] + [VMEM] * 4 + [ANY] * (1 + len(coded) + len(tokens)),
        out_specs=[VMEM] * (len(out_slots) + 1),
        out_shape=out_shape,
        scratch_shapes=[
            pltpu.VMEM((terms, 2 * tile, tile), jnp.bfloat16),
            pltpu.VMEM((sum(len(slots) for slots in out_slots), tile, tile), jnp.float32),
            pltpu.VMEM((terms, tile, tile), jnp.bfloat16),
            pltpu.SemaphoreType.DMA,
            pltpu.VMEM((2, CODE_ROWS, tile), jnp.bfloat16),
            pltpu.SemaphoreType.DMA((2,)),
        ],
        compiler_params=pltpu.CompilerParams(vmem_limit_bytes=held + 4 * MIB),
        cost_estimate=BRIEF,
    )(source, target, blocks, *left, right[first], *coded, *tokens)


def encode(values):
    rows = lax.broadcasted_iota(jnp.int32, (CODE_ROWS, 256), 0)
    out = jnp.zeros((CODE_ROWS, 256), jnp.float32)
    for at, value in enumerate(values):
        rest = jnp.broadcast_to(value, out.shape)
        for part in range(3):
            head = rest.astype(jnp.bfloat16).astype(jnp.float32)
            out = jnp.where(rows == 3 * at + part, head, out)
            rest = rest - head
    return out.astype(jnp.bfloat16)


def decode(code):
    code = code[:6, :1].astype(jnp.float32)
    return [code[at:at + 1] + code[at + 1:at + 2] + code[at + 2:at + 3] for at in (0, 3)]


def combine_kernel(first, local, left_sizes, right_sizes, kept, arrived, blocks, *refs):
    before = refs[0]
    both, near, stats, held, sem = refs[-5:]
    tile = near.shape[0]
    copy = pltpu.make_async_copy(blocks.at[first], held, sem)
    copy.start()
    row, col = lax.axis_index("row"), lax.axis_index("col")
    image = kept[...] + arrived[...].astype(jnp.float32)
    both[:2 * tile] = image.astype(both.dtype)
    near[...] = image[tile:].astype(near.dtype)
    copy.wait()
    norm = correlation = jnp.zeros((8, tile), jnp.float32)
    for slot in range(2):
        rows = pl.ds(slot * tile, tile)
        masked = keep_corner(held[rows], left_sizes[lax.bitwise_xor(row, slot)], right_sizes[col * local + first])
        masked = masked.astype(jnp.float32)
        norm += jnp.sum((masked * masked).reshape(-1, 8, tile), 0)
        correlation += jnp.sum((masked * image[slot * tile:(slot + 1) * tile]).reshape(-1, 8, tile), 0)
    if first:
        norm, correlation = norm + before[0], correlation + before[1]
    stats[0] = norm
    stats[1] = correlation
    if first == local - 1:
        both[2 * tile:] = encode([jnp.sum(norm), jnp.sum(correlation)])


def combine(first, local, left_sizes, right_sizes, kept, arrived, blocks, stats, tokens):
    tile = kept.shape[1]
    rows = 2 * tile + CODE_ROWS * (first == local - 1)
    more = ([stats] if first else []) + tokens
    return pl.pallas_call(
        functools.partial(combine_kernel, first, local),
        in_specs=[SMEM, SMEM, VMEM, VMEM, ANY] + ([VMEM] if first else []) + [ANY] * len(tokens),
        out_specs=[VMEM] * 3,
        out_shape=[jax.ShapeDtypeStruct((height, tile), arrived.dtype) for height in (rows, tile)]
        + [jax.ShapeDtypeStruct((2, 8, tile), jnp.float32)],
        scratch_shapes=[pltpu.VMEM((2 * tile, tile), blocks.dtype), pltpu.SemaphoreType.DMA],
        compiler_params=pltpu.CompilerParams(vmem_limit_bytes=VMEM_LIMIT),
        cost_estimate=BRIEF,
    )(left_sizes, right_sizes, kept, arrived, blocks, *more)


def emit_kernel(start, coded, kept, arrived, *refs):
    outs = refs[-1 - coded:]
    tile = kept.shape[1]
    outs[0][:tile] = (kept[tile:] + arrived[start:start + tile].astype(jnp.float32)).astype(outs[0].dtype)
    if coded:
        more = decode(arrived[arrived.shape[0] - CODE_ROWS:])
        stats = [refs[0][at, :1, :1] + more[at] for at in range(2)]
        outs[0][tile:] = encode(stats)
        for at, value in enumerate(stats):
            outs[1][at] = jnp.broadcast_to(value, outs[1].shape[1:])


def emit(kept, arrived, tokens, stats=None):
    tile, coded = kept.shape[1], stats is not None
    start = tile if arrived.shape[0] >= 2 * tile else 0
    return pl.pallas_call(
        functools.partial(emit_kernel, start, coded),
        in_specs=[VMEM] * (2 + coded) + [ANY] * len(tokens),
        out_specs=[VMEM] * (1 + coded),
        out_shape=[jax.ShapeDtypeStruct((tile + CODE_ROWS * coded, tile), arrived.dtype)] + [TOKEN] * coded,
        compiler_params=pltpu.CompilerParams(vmem_limit_bytes=VMEM_LIMIT),
        cost_estimate=BRIEF,
    )(kept, arrived, *([stats] if coded else []), *tokens)


def finish_kernel(entry_count, local, carrier, stats, *refs):
    parts, near_images, kept, arrived, near_again = (refs[at * local:(at + 1) * local] for at in range(5))
    outs, (image_held, kept_held, more_held, out_held, code, sems, out_sems) = refs[5 * local:5 * local + 2], refs[-7:]
    tile = image_held.shape[1]
    leading = leads(lax.axis_index("row")) == 1

    def own(first):
        pairs = [(parts, image_held), (arrived, more_held), (kept, kept_held)]
        return [
            pltpu.make_async_copy(source[first].at[:tile], held.at[first], sems.at[at, first])
            for at, (source, held) in enumerate(pairs)
        ]

    def sent(first):
        pairs = [(near_images, image_held), (near_again, more_held)]
        copies = [
            pltpu.make_async_copy(source[first].at[:tile], held.at[first], sems.at[at, first])
            for at, (source, held) in enumerate(pairs)
        ]
        if first == carrier:
            copies.append(pltpu.make_async_copy(near_again[first].at[tile:], code, sems.at[2, first]))
        return copies

    def each(firsts, act):
        for first in firsts:
            @pl.when(leading)
            def _():
                for copy in own(first):
                    act(copy)

            @pl.when(jnp.logical_not(leading))
            def _():
                for copy in sent(first):
                    act(copy)

    order = [first for first in range(local) if first == carrier] + [first for first in range(local) if first != carrier]
    each(order, lambda copy: copy.start())
    scale = theta = None
    out_copies = []
    for first in order:
        each([first], lambda copy: copy.wait())
        if scale is None:
            norm, correlation = stats[0, :1, :1], stats[1, :1, :1]
            if carrier < local:
                norm, correlation = (
                    jnp.where(leading, mine, theirs) for mine, theirs in zip((norm, correlation), decode(code[...]))
                )
            scale = lax.rsqrt(norm / entry_count + 1e-06)
            theta = correlation / norm
        image = image_held[first].astype(jnp.float32)
        value = jnp.where(leading, kept_held[first], 0.0) + more_held[first].astype(jnp.float32)
        out_held[0, first] = (image * scale).astype(out_held.dtype)
        out_held[1, first] = ((value - theta * image) * scale).astype(out_held.dtype)
        for at, out in enumerate(outs):
            copy = pltpu.make_async_copy(
                out_held.at[at, first], out.at[:, first * tile:(first + 1) * tile], out_sems.at[at, first]
            )
            copy.start()
            out_copies.append(copy)
    for copy in out_copies:
        copy.wait()


def finish(entry_count, carrier, stats, parts, near_images, again, near_again):
    local, tile = len(parts), near_images[0].shape[0]
    out = jax.ShapeDtypeStruct((tile, local * tile), near_images[0].dtype)
    block = (local, tile, tile)
    return pl.pallas_call(
        functools.partial(finish_kernel, entry_count, local, carrier),
        in_specs=[VMEM] + [ANY] * (5 * local),
        out_specs=[ANY, ANY],
        out_shape=[out, out],
        scratch_shapes=[
            pltpu.VMEM(block, out.dtype),
            pltpu.VMEM(block, jnp.float32),
            pltpu.VMEM(block, out.dtype),
            pltpu.VMEM((2, *block), out.dtype),
            pltpu.VMEM((CODE_ROWS, tile), out.dtype),
            pltpu.SemaphoreType.DMA((3, local)),
            pltpu.SemaphoreType.DMA((2, local)),
        ],
        compiler_params=pltpu.CompilerParams(vmem_limit_bytes=VMEM_LIMIT),
        cost_estimate=BRIEF,
    )(stats, *parts, *near_images, *(kept for kept, _ in again), *(arrived[0] for _, arrived in again), *near_again)


def after(value, *others):
    return pl.pallas_call(
        lambda *refs: None,
        in_specs=[ANY] * (1 + len(others)),
        out_specs=ANY,
        out_shape=jax.ShapeDtypeStruct(value.shape, value.dtype),
        input_output_aliases={0: 0},
        cost_estimate=BRIEF,
    )(value, *others)


def on_device(wavefunction, left_ops, right_ops, left_dest, right_src, left_sizes, right_sizes):
    tile = left_ops.shape[2]
    local = right_ops.shape[1]
    row_count, col_count = lax.axis_size("row"), lax.axis_size("col")
    pair_bits, col_bits = bits_of(row_count) - 1, bits_of(col_count)
    entry_count = wavefunction.shape[0] * row_count * wavefunction.shape[1] * col_count
    both = ("row", "col")
    row, col = lax.axis_index("row"), lax.axis_index("col")
    leading = leads(row) == 1
    blocks_shape = (col_count * local, 2 * tile, tile)

    def far(part):
        pieces = [part]
        for bit in range(1, col_bits):
            pieces += [lax.ppermute(piece, "col", swap("col", 1 << bit)) for piece in pieces]
        return pieces

    def other_core(part):
        return lax.ppermute(part, "col", swap("col", 1))

    def block_of(piece, odd):
        return (odd * (col_count // 2) + piece) * local

    def to_partner(part):
        return lax.ppermute(part, "row", swap("row", 1))

    near = to_partner(wavefunction)
    left_own, left_near = mask_left(left_dest, left_sizes, left_ops)
    left_near = to_partner(left_near)
    left = [left_own, left_near, other_core(left_near)]
    right = mask_right(right_src, right_sizes, right_ops)
    near = after(near, left_own, right[0])

    def exchange(sums):
        kept, sums = sums[0], sums[1:]
        per_pair = len(sums) // ((1 << pair_bits) - 1)
        for bit in range(pair_bits):
            half = (len(sums) + per_pair) // 2 - per_pair
            arrived = [lax.ppermute(part, both, leader_swap(1 << bit)) for part in sums[half:][::-1]][::-1]
            if bit < pair_bits - 1:
                mine = arrived[0] if per_pair == 1 else jnp.concatenate(arrived[:per_pair], 0)
                kept = kept + mine.astype(jnp.float32)
                sums = [
                    (part.astype(jnp.float32) + more.astype(jnp.float32)).astype(part.dtype)
                    for part, more in zip(sums[:half], arrived[per_pair:])
                ]
        return kept, arrived

    joined = [(2 * pair, 2 * pair + 1) for pair in range(1 << pair_bits)]
    apart = joined[:1] + [(slot,) for pair in joined[1:] for slot in pair]

    def multiply(blocks, slots, first, tokens, coded=()):
        return products(blocks, left, right, right_src, left_dest, slots, first, tokens, coded)

    pieces = [((block_of(at, 0), 0), piece) for at, piece in enumerate(far(wavefunction))]
    near_pieces = [((block_of(at, 0), 1), piece) for at, piece in enumerate(far(near))]
    blocks = None
    for several in (pieces + near_pieces[:1], near_pieces[1:]):
        blocks = place(blocks, blocks_shape, several + [
            ((block + block_of(0, 1), slot), other_core(piece)) for (block, slot), piece in several
        ])

    once, parts, near_images, stats, token = [], [], [], None, None
    for first in range(local + 1):
        if first < local:
            *sums, token = multiply(blocks, joined, first, ([token] if first else []) + ([stats] if parts else []))
            once.append(exchange(sums))
        for done in range(len(parts), first if first < local else local):
            kept, (arrived,) = once[done]
            image, near_image, stats = combine(
                done, local, left_sizes, right_sizes, kept, arrived, blocks, stats,
                [token] + (parts[0][1:] if done > 1 else []),
            )
            parts.append(far(image))
            near_images.append(to_partner(near_image))
    blocks = None
    for group in (range(local - 1), range(local - 1, local)):
        if blocks is None:
            held = place(
                None,
                (len(group) * col_count // 2, 2 * tile, tile),
                [((at * len(group) + i, 0), parts[first][at]) for at in range(col_count // 2) for i, first in enumerate(group)],
                [parts[-1][0], *near_images[:-2]],
            )
        else:
            held = join(parts[-1], [blocks, *near_images[-2:]])
        arrived_held = other_core(held)
        blocks = place(blocks, blocks_shape, [
            ((block_of(at, odd) + group[0], 0), half[at * len(group):(at + 1) * len(group)])
            for odd, half in enumerate((held, arrived_held))
            for at in range(col_count // 2)
        ])

    carrier = local - 2 if pair_bits == 1 else local
    again, near_again, token, stats = [], [], None, None
    for first in range(local + 1):
        if first < local:
            slots = apart if first == local - 1 else joined
            tokens = ([token] if first else []) + ([near_again[-1]] if near_again else [])
            coded = [held, arrived_held] if first == carrier else []
            *sums, token = multiply(blocks, slots, first, tokens, coded)
            stats = token if coded else stats
            again.append(exchange(sums))
        for done in range(len(near_again), first if first < local else local):
            kept, arrived = again[done]
            tokens = [token]
            if done == carrier:
                near, stats = emit(kept, arrived[-1], tokens, stats)
            else:
                (near,) = emit(kept, arrived[-1], tokens)
            near_again.append(near)
    near_again = [to_partner(part) for part in near_again]
    if carrier == local:
        stats = settle(held, arrived_held, [token])
        for bit in range(pair_bits):
            stats = stats + lax.ppermute(stats, both, leader_swap(1 << bit))
        stats = jnp.where(leading, stats, to_partner(stats))
    return tuple(finish(entry_count, carrier, stats, [part[0] for part in parts], near_images, again, near_again))


def solution(mesh):
    placed = (
        P(("groups", "row"), "col"),
        P(None, ("groups", "row"), None, None),
        P(None, ("groups", "col"), None, None),
        P(None, "groups"),
        P(None, "groups"),
        P("groups"),
        P("groups"),
    )
    return jax.shard_map(
        on_device,
        mesh=mesh,
        in_specs=placed,
        out_specs=(P(("groups", "row"), "col"), P(("groups", "row"), "col")),
        check_vma=False,
    )
```

```python
import functools

import jax
import jax.numpy as jnp
from jax import lax
from jax.experimental import pallas as pl
from jax.experimental.pallas import tpu as pltpu
from jax.sharding import PartitionSpec as P

MIB = 1024 * 1024
CODE_ROWS = 16
VMEM_LIMIT = 10 * MIB
MASK_LIMIT = 60 * MIB
ANY = pl.BlockSpec(memory_space=pl.ANY)
BRIEF = pl.CostEstimate(flops=10**9, bytes_accessed=0, transcendentals=0)
TOKEN = jax.ShapeDtypeStruct((2, 8, 128), jnp.float32)
VMEM = pl.BlockSpec(memory_space=pltpu.VMEM)
SMEM = pl.BlockSpec(memory_space=pltpu.SMEM)


def bits_of(size):
    count = size.bit_length() - 1
    assert 1 << count == size
    return count


def swap(axis, bit):
    return [(place, place ^ bit) for place in range(lax.axis_size(axis))]


def leads(row):
    return (row ^ (row >> 1)) & 1


def leader_swap(bit):
    rows, cols = lax.axis_size("row"), lax.axis_size("col")
    pairs = []
    for row in range(rows):
        for col in range(cols):
            if leads(row):
                pair = (row >> 1) ^ bit
                there = (2 * pair if leads(2 * pair) else 2 * pair + 1, col)
            else:
                there = (row, col ^ 1)
            pairs.append((row * cols + col, there[0] * cols + there[1]))
    return pairs


def reverse_bits(value, count):
    out = 0
    for bit in range(count):
        out = out | (((value >> bit) & 1) << (count - 1 - bit))
    return out


def keep_corner(block, rows, cols):
    inside = (lax.broadcasted_iota(jnp.int32, block.shape, 0) < rows) & (
        lax.broadcasted_iota(jnp.int32, block.shape, 1) < cols
    )
    return jnp.where(inside, block.astype(jnp.float32), 0.0).astype(block.dtype)


def mask_left_kernel(left_dest, left_sizes, left, out, near, token):
    token[...] = jnp.zeros_like(token)
    row, col = lax.axis_index("row"), lax.axis_index("col")
    terms, half = out.shape[0], near.shape[0]
    for term in range(terms):
        out[term] = keep_corner(left[term, 0], left_sizes[left_dest[term, row]], left_sizes[row])
    for place in range(half):
        near[place] = out[lax.rem(col, 2) * half + place]


def mask_left(left_dest, left_sizes, left):
    terms, _, tile, _ = left.shape
    return pl.pallas_call(
        mask_left_kernel,
        in_specs=[SMEM, SMEM, VMEM],
        out_specs=[VMEM] * 3,
        out_shape=[jax.ShapeDtypeStruct((count, tile, tile), left.dtype) for count in (terms, terms // 2)] + [TOKEN],
        compiler_params=pltpu.CompilerParams(vmem_limit_bytes=MASK_LIMIT),
        cost_estimate=BRIEF,
    )(left_dest, left_sizes, left)


def mask_right_kernel(right_src, right_sizes, right, *outs):
    *outs, token = outs
    token[...] = jnp.zeros_like(token)
    col = lax.axis_index("col")
    for step in range(right.shape[0]):
        term = pl.program_id(0) * right.shape[0] + step
        for place, out in enumerate(outs):
            block = col * len(outs) + place
            out[step] = keep_corner(right[step, place], right_sizes[block], right_sizes[right_src[term, block]])


def mask_right(right_src, right_sizes, right):
    terms, local, tile, _ = right.shape
    return pl.pallas_call(
        mask_right_kernel,
        grid=(terms // 2,),
        in_specs=[SMEM, SMEM, pl.BlockSpec((2, local, tile, tile), lambda step: (step, 0, 0, 0))],
        out_specs=[pl.BlockSpec((2, tile, tile), lambda step: (step, 0, 0))] * local
        + [pl.BlockSpec(TOKEN.shape, lambda step: (0, 0, 0))],
        out_shape=[jax.ShapeDtypeStruct((terms, tile, tile), right.dtype)] * local + [TOKEN],
        compiler_params=pltpu.CompilerParams(vmem_limit_bytes=MASK_LIMIT),
        cost_estimate=BRIEF,
    )(right_src, right_sizes, right)


def place_kernel(places, *refs):
    pieces, (blocks, sems) = refs[:len(places)], refs[-2:]
    tile = blocks.shape[2]
    copies = []

    def add(here, there):
        copies.append(pltpu.make_async_copy(here, there, sems.at[len(copies)]))

    for (block, slot), piece in zip(places, pieces):
        if len(piece.shape) == 3:
            add(piece.at[:, :blocks.shape[1]], blocks.at[block:block + piece.shape[0]])
        else:
            for at in range(piece.shape[1] // tile):
                rows = piece.shape[0]
                add(piece.at[:, at * tile:(at + 1) * tile], blocks.at[block + at, slot * tile:slot * tile + rows])
    for copy in copies:
        copy.start()
    for copy in copies:
        copy.wait()


def place(blocks, shape, pieces, tokens=()):
    places, pieces = [at for at, _ in pieces], [piece for _, piece in pieces]
    copies = sum(1 if piece.ndim == 3 else piece.shape[1] // shape[2] for piece in pieces)
    rest = list(tokens) if blocks is None else [blocks, *tokens]
    return pl.pallas_call(
        functools.partial(place_kernel, places),
        in_specs=[ANY] * (len(pieces) + len(rest)),
        out_specs=ANY,
        out_shape=jax.ShapeDtypeStruct(shape, jnp.bfloat16),
        scratch_shapes=[pltpu.SemaphoreType.DMA((copies,))],
        input_output_aliases={} if blocks is None else {len(pieces): 0},
        compiler_params=pltpu.CompilerParams(vmem_limit_bytes=VMEM_LIMIT),
        cost_estimate=BRIEF,
    )(*pieces, *rest)


def join_kernel(*refs):
    held, pieces = refs[-1], refs[:refs[-1].shape[0]]
    rows = held.shape[1] - CODE_ROWS
    sums = [jnp.zeros((1, 1), jnp.float32)] * 2
    for at, piece in enumerate(pieces):
        held[at, :rows] = piece[:rows]
        sums = [total + more for total, more in zip(sums, decode(piece[rows:]))]
        if at:
            held[at, rows:] = jnp.zeros((CODE_ROWS, held.shape[2]), held.dtype)
    held[0, rows:] = encode(sums)


def join(pieces, tokens):
    return pl.pallas_call(
        join_kernel,
        in_specs=[VMEM] * len(pieces) + [ANY] * len(tokens),
        out_specs=VMEM,
        out_shape=jax.ShapeDtypeStruct((len(pieces), *pieces[0].shape), pieces[0].dtype),
        compiler_params=pltpu.CompilerParams(vmem_limit_bytes=VMEM_LIMIT),
        cost_estimate=BRIEF,
    )(*pieces, *tokens)


def read_codes(arrays, codes, sems):
    copies = [
        pltpu.make_async_copy(ref.at[0, ref.shape[1] - CODE_ROWS:], codes.at[at], sems.at[at])
        for at, ref in enumerate(arrays)
    ]
    for copy in copies:
        copy.start()
    for copy in copies:
        copy.wait()
    return jnp.stack([jnp.broadcast_to(sum(pair), (8, 128)) for pair in zip(decode(codes[0]), decode(codes[1]))])


def settle_kernel(held, arrived, *refs):
    out, codes, sems = refs[-3:]
    out[...] = read_codes((held, arrived), codes, sems)


def settle(held, arrived, tokens):
    return pl.pallas_call(
        settle_kernel,
        in_specs=[ANY] * (2 + len(tokens)),
        out_specs=VMEM,
        out_shape=jax.ShapeDtypeStruct((2, 8, 128), jnp.float32),
        scratch_shapes=[pltpu.VMEM((2, CODE_ROWS, held.shape[2]), held.dtype), pltpu.SemaphoreType.DMA((2,))],
        compiler_params=pltpu.CompilerParams(vmem_limit_bytes=VMEM_LIMIT),
        cost_estimate=BRIEF,
    )(held, arrived, *tokens)


def product_kernel(first, local, out_slots, coded, source, target, blocks, left_own, left_near, left_far, right, *refs):
    outs, (token, inner, total, held_right, sem, codes, code_sems) = refs[-7 - len(out_slots):-7], refs[-7:]
    pair_count = total.shape[0] // 2
    if coded:
        token[...] = read_codes(refs[:2], codes, code_sems)
    else:
        token[...] = jnp.zeros_like(token)
    copy = pltpu.make_async_copy(right, held_right, sem)
    copy.start()
    total[...] = jnp.zeros_like(total)
    copy.wait()
    terms, tile = right.shape[:2]
    row, col = lax.axis_index("row"), lax.axis_index("col")
    for term in range(terms):
        wanted = source[term, col * local + first]
        place_of = lax.bitwise_xor(lax.div(wanted, local), col)
        place_of = (place_of >> 1) + (place_of & 1) * (blocks.shape[0] // local // 2)
        held = place_of * local + lax.rem(wanted, local)
        inner[term] = lax.dot_general(
            blocks[held], held_right[term], (((1,), (1,)), ((), ())), preferred_element_type=jnp.float32
        ).astype(jnp.bfloat16)

    def add(left, term, slot):
        to = target[term, lax.bitwise_xor(row, slot)]
        to_slot = 2 * reverse_bits((to >> 1) ^ (row >> 1), bits_of(pair_count)) + 1 - leads(to)
        total[to_slot] += jnp.dot(left, inner[term, slot * tile:(slot + 1) * tile], preferred_element_type=jnp.float32)

    half = terms // 2
    near = lax.rem(col, 2) * half
    for term in range(terms):
        add(left_own[term], term, 0)
    for step in range(half):
        add(left_near[step], near + step, 1)
        add(left_far[step], half - near + step, 1)
    for slots, out in zip(out_slots, outs):
        for at, slot in enumerate(slots):
            out[at * tile:(at + 1) * tile] = total[slot].astype(out.dtype)
        if coded and slots[0] >= 2:
            out[len(slots) * tile:] = encode([token[0, :1, :1], token[1, :1, :1]])


def products(blocks, left, right, source, target, out_slots, first, tokens, coded=()):
    local, (terms, tile) = len(right), right[0].shape[:2]
    out_shape = [
        jax.ShapeDtypeStruct((len(slots) * tile + CODE_ROWS, tile), jnp.bfloat16)
        if coded and slots[0] >= 2
        else jax.ShapeDtypeStruct((len(slots) * tile, tile), jnp.bfloat16 if slots[0] >= 2 else jnp.float32)
        for slots in out_slots
    ] + [TOKEN]
    held = 2 * blocks.size + 8 * terms * tile * tile + sum(8 * out.size for out in out_shape)
    return pl.pallas_call(
        functools.partial(product_kernel, first, local, out_slots, bool(coded)),
        in_specs=[SMEM, SMEM] + [VMEM] * 4 + [ANY] * (1 + len(coded) + len(tokens)),
        out_specs=[VMEM] * (len(out_slots) + 1),
        out_shape=out_shape,
        scratch_shapes=[
            pltpu.VMEM((terms, 2 * tile, tile), jnp.bfloat16),
            pltpu.VMEM((sum(len(slots) for slots in out_slots), tile, tile), jnp.float32),
            pltpu.VMEM((terms, tile, tile), jnp.bfloat16),
            pltpu.SemaphoreType.DMA,
            pltpu.VMEM((2, CODE_ROWS, tile), jnp.bfloat16),
            pltpu.SemaphoreType.DMA((2,)),
        ],
        compiler_params=pltpu.CompilerParams(vmem_limit_bytes=held + 4 * MIB),
        cost_estimate=BRIEF,
    )(source, target, blocks, *left, right[first], *coded, *tokens)


def encode(values):
    rows = lax.broadcasted_iota(jnp.int32, (CODE_ROWS, 256), 0)
    out = jnp.zeros((CODE_ROWS, 256), jnp.float32)
    for at, value in enumerate(values):
        rest = jnp.broadcast_to(value, out.shape)
        for part in range(3):
            head = rest.astype(jnp.bfloat16).astype(jnp.float32)
            out = jnp.where(rows == 3 * at + part, head, out)
            rest = rest - head
    return out.astype(jnp.bfloat16)


def decode(code):
    code = code[:6, :1].astype(jnp.float32)
    return [code[at:at + 1] + code[at + 1:at + 2] + code[at + 2:at + 3] for at in (0, 3)]


def combine_kernel(first, local, left_sizes, right_sizes, kept, arrived, blocks, *refs):
    before = refs[0]
    both, near, stats, held, sem = refs[-5:]
    tile = near.shape[0]
    copy = pltpu.make_async_copy(blocks.at[first], held, sem)
    copy.start()
    row, col = lax.axis_index("row"), lax.axis_index("col")
    image = kept[...] + arrived[...].astype(jnp.float32)
    both[:2 * tile] = image.astype(both.dtype)
    near[...] = image[tile:].astype(near.dtype)
    copy.wait()
    norm = correlation = jnp.zeros((8, tile), jnp.float32)
    for slot in range(2):
        rows = pl.ds(slot * tile, tile)
        masked = keep_corner(held[rows], left_sizes[lax.bitwise_xor(row, slot)], right_sizes[col * local + first])
        masked = masked.astype(jnp.float32)
        norm += jnp.sum((masked * masked).reshape(-1, 8, tile), 0)
        correlation += jnp.sum((masked * image[slot * tile:(slot + 1) * tile]).reshape(-1, 8, tile), 0)
    if first:
        norm, correlation = norm + before[0], correlation + before[1]
    stats[0] = norm
    stats[1] = correlation
    if first == local - 1:
        both[2 * tile:] = encode([jnp.sum(norm), jnp.sum(correlation)])


def combine(first, local, left_sizes, right_sizes, kept, arrived, blocks, stats, tokens):
    tile = kept.shape[1]
    rows = 2 * tile + CODE_ROWS * (first == local - 1)
    more = ([stats] if first else []) + tokens
    return pl.pallas_call(
        functools.partial(combine_kernel, first, local),
        in_specs=[SMEM, SMEM, VMEM, VMEM, ANY] + ([VMEM] if first else []) + [ANY] * len(tokens),
        out_specs=[VMEM] * 3,
        out_shape=[jax.ShapeDtypeStruct((height, tile), arrived.dtype) for height in (rows, tile)]
        + [jax.ShapeDtypeStruct((2, 8, tile), jnp.float32)],
        scratch_shapes=[pltpu.VMEM((2 * tile, tile), blocks.dtype), pltpu.SemaphoreType.DMA],
        compiler_params=pltpu.CompilerParams(vmem_limit_bytes=VMEM_LIMIT),
        cost_estimate=BRIEF,
    )(left_sizes, right_sizes, kept, arrived, blocks, *more)


def emit_kernel(start, coded, kept, arrived, *refs):
    outs = refs[-1 - coded:]
    tile = kept.shape[1]
    outs[0][:tile] = (kept[tile:] + arrived[start:start + tile].astype(jnp.float32)).astype(outs[0].dtype)
    if coded:
        more = decode(arrived[arrived.shape[0] - CODE_ROWS:])
        stats = [refs[0][at, :1, :1] + more[at] for at in range(2)]
        outs[0][tile:] = encode(stats)
        for at, value in enumerate(stats):
            outs[1][at] = jnp.broadcast_to(value, outs[1].shape[1:])


def emit(kept, arrived, tokens, stats=None):
    tile, coded = kept.shape[1], stats is not None
    start = tile if arrived.shape[0] >= 2 * tile else 0
    return pl.pallas_call(
        functools.partial(emit_kernel, start, coded),
        in_specs=[VMEM] * (2 + coded) + [ANY] * len(tokens),
        out_specs=[VMEM] * (1 + coded),
        out_shape=[jax.ShapeDtypeStruct((tile + CODE_ROWS * coded, tile), arrived.dtype)] + [TOKEN] * coded,
        compiler_params=pltpu.CompilerParams(vmem_limit_bytes=VMEM_LIMIT),
        cost_estimate=BRIEF,
    )(kept, arrived, *([stats] if coded else []), *tokens)


def finish_kernel(entry_count, local, carrier, stats, *refs):
    parts, near_images, kept, arrived, near_again = (refs[at * local:(at + 1) * local] for at in range(5))
    outs, (image_held, kept_held, more_held, out_held, code, sems, out_sems) = refs[-9:-7], refs[-7:]
    tile = image_held.shape[1]
    leading = leads(lax.axis_index("row")) == 1

    def own(first):
        pairs = [(parts, image_held), (arrived, more_held), (kept, kept_held)]
        return [
            pltpu.make_async_copy(source[first].at[:tile], held.at[first], sems.at[at, first])
            for at, (source, held) in enumerate(pairs)
        ]

    def sent(first):
        pairs = [(near_images, image_held), (near_again, more_held)]
        copies = [
            pltpu.make_async_copy(source[first].at[:tile], held.at[first], sems.at[at, first])
            for at, (source, held) in enumerate(pairs)
        ]
        if first == carrier:
            copies.append(pltpu.make_async_copy(near_again[first].at[tile:], code, sems.at[2, first]))
        return copies

    def each(firsts, act):
        for first in firsts:
            @pl.when(leading)
            def _():
                for copy in own(first):
                    act(copy)

            @pl.when(jnp.logical_not(leading))
            def _():
                for copy in sent(first):
                    act(copy)

    order = [first for first in range(local) if first == carrier] + [first for first in range(local) if first != carrier]
    each(order, lambda copy: copy.start())
    scale = theta = None
    out_copies = []
    for first in order:
        each([first], lambda copy: copy.wait())
        if scale is None:
            norm, correlation = stats[0, :1, :1], stats[1, :1, :1]
            if carrier < local:
                norm, correlation = (
                    jnp.where(leading, mine, theirs) for mine, theirs in zip((norm, correlation), decode(code[...]))
                )
            scale = lax.rsqrt(norm / entry_count + 1e-06)
            theta = correlation / norm
        image = image_held[first].astype(jnp.float32)
        value = jnp.where(leading, kept_held[first], 0.0) + more_held[first].astype(jnp.float32)
        out_held[0, first] = (image * scale).astype(out_held.dtype)
        out_held[1, first] = ((value - theta * image) * scale).astype(out_held.dtype)
        for at, out in enumerate(outs):
            copy = pltpu.make_async_copy(
                out_held.at[at, first], out.at[:, first * tile:(first + 1) * tile], out_sems.at[at, first]
            )
            copy.start()
            out_copies.append(copy)
    for copy in out_copies:
        copy.wait()


def finish(entry_count, carrier, stats, parts, near_images, again, near_again, tokens):
    local, tile = len(parts), near_images[0].shape[0]
    out = jax.ShapeDtypeStruct((tile, local * tile), near_images[0].dtype)
    block = (local, tile, tile)
    return pl.pallas_call(
        functools.partial(finish_kernel, entry_count, local, carrier),
        in_specs=[VMEM] + [ANY] * (5 * local + len(tokens)),
        out_specs=[ANY, ANY],
        out_shape=[out, out],
        scratch_shapes=[
            pltpu.VMEM(block, out.dtype),
            pltpu.VMEM(block, jnp.float32),
            pltpu.VMEM(block, out.dtype),
            pltpu.VMEM((2, *block), out.dtype),
            pltpu.VMEM((CODE_ROWS, tile), out.dtype),
            pltpu.SemaphoreType.DMA((3, local)),
            pltpu.SemaphoreType.DMA((2, local)),
        ],
        compiler_params=pltpu.CompilerParams(vmem_limit_bytes=VMEM_LIMIT),
        cost_estimate=BRIEF,
    )(stats, *parts, *near_images, *(kept for kept, _ in again), *(arrived[0] for _, arrived in again), *near_again, *tokens)


def after_kernel(value, *refs):
    refs[-1][...] = value[...]


def after(value, *others):
    return pl.pallas_call(
        after_kernel,
        in_specs=[VMEM] + [ANY] * len(others),
        out_specs=VMEM,
        out_shape=jax.ShapeDtypeStruct(value.shape, value.dtype),
        compiler_params=pltpu.CompilerParams(vmem_limit_bytes=VMEM_LIMIT),
        cost_estimate=BRIEF,
    )(value, *others)


def arrive_kernel(*refs):
    refs[-1][...] = jnp.zeros_like(refs[-1])


def arrive(cost, *values):
    return pl.pallas_call(
        arrive_kernel,
        in_specs=[ANY] * len(values),
        out_specs=VMEM,
        out_shape=TOKEN,
        compiler_params=pltpu.CompilerParams(vmem_limit_bytes=VMEM_LIMIT),
        cost_estimate=pl.CostEstimate(flops=cost, bytes_accessed=0, transcendentals=0),
    )(*values)


def on_device(wavefunction, left_ops, right_ops, left_dest, right_src, left_sizes, right_sizes):
    tile = left_ops.shape[2]
    local = right_ops.shape[1]
    row_count, col_count = lax.axis_size("row"), lax.axis_size("col")
    pair_bits, col_bits = bits_of(row_count) - 1, bits_of(col_count)
    entry_count = wavefunction.shape[0] * row_count * wavefunction.shape[1] * col_count
    both = ("row", "col")
    row, col = lax.axis_index("row"), lax.axis_index("col")
    leading = leads(row) == 1
    blocks_shape = (col_count * local, 2 * tile, tile)

    def far(part):
        pieces = [part]
        for bit in range(1, col_bits):
            pieces += [lax.ppermute(piece, "col", swap("col", 1 << bit)) for piece in pieces]
        return pieces

    def other_core(part):
        return lax.ppermute(part, "col", swap("col", 1))

    def block_of(piece, odd):
        return (odd * (col_count // 2) + piece) * local

    def to_partner(part):
        return lax.ppermute(part, "row", swap("row", 1))

    near = to_partner(wavefunction)
    left_own, left_near, left_token = mask_left(left_dest, left_sizes, left_ops)
    left_near = to_partner(left_near)
    left = [left_own, left_near, other_core(left_near)]
    *right, right_token = mask_right(right_src, right_sizes, right_ops)
    near = after(near, left_token, right_token)

    def exchange(sums):
        kept, sums = sums[0], sums[1:]
        per_pair = len(sums) // ((1 << pair_bits) - 1)
        for bit in range(pair_bits):
            half = (len(sums) + per_pair) // 2 - per_pair
            arrived = [lax.ppermute(part, both, leader_swap(1 << bit)) for part in sums[half:][::-1]][::-1]
            if bit < pair_bits - 1:
                mine = arrived[0] if per_pair == 1 else jnp.concatenate(arrived[:per_pair], 0)
                kept = kept + mine.astype(jnp.float32)
                sums = [
                    (part.astype(jnp.float32) + more.astype(jnp.float32)).astype(part.dtype)
                    for part, more in zip(sums[:half], arrived[per_pair:])
                ]
        return kept, arrived

    joined = [(2 * pair, 2 * pair + 1) for pair in range(1 << pair_bits)]
    apart = joined[:1] + [(slot,) for pair in joined[1:] for slot in pair]

    def multiply(blocks, slots, first, tokens, coded=()):
        return products(blocks, left, right, right_src, left_dest, slots, first, tokens, coded)

    left_there = arrive(2 * 10**9, left[2])

    pieces = [((block_of(at, 0), 0), piece) for at, piece in enumerate(far(wavefunction))]
    near_pieces = [((block_of(at, 0), 1), piece) for at, piece in enumerate(far(near))]
    blocks = None
    for several in (pieces + near_pieces[:1], near_pieces[1:]):
        blocks = place(blocks, blocks_shape, several + [
            ((block + block_of(0, 1), slot), other_core(piece)) for (block, slot), piece in several
        ])

    once, parts, near_images, stats, token = [], [], [], None, None
    for first in range(local + 1):
        if first < local:
            *sums, token = multiply(blocks, joined, first, ([token] if first else [left_there]) + ([stats] if parts else []))
            once.append(exchange(sums))
        for done in range(len(parts), first if first < local else local):
            kept, (arrived,) = once[done]
            image, near_image, stats = combine(
                done, local, left_sizes, right_sizes, kept, arrived, blocks, stats,
                [token] + (parts[0][1:] if done > 1 else []),
            )
            parts.append(far(image))
            near_images.append(to_partner(near_image))
    blocks = None
    for group in (range(local - 1), range(local - 1, local)):
        if blocks is None:
            held = place(
                None,
                (len(group) * col_count // 2, 2 * tile, tile),
                [((at * len(group) + i, 0), parts[first][at]) for at in range(col_count // 2) for i, first in enumerate(group)],
                [parts[-1][0], *near_images[:-2]],
            )
        else:
            held = join(parts[-1], [blocks, near_images[-2]])
        arrived_held = other_core(held)
        blocks = place(blocks, blocks_shape, [
            ((block_of(at, odd) + group[0], 0), half[at * len(group):(at + 1) * len(group)])
            for odd, half in enumerate((held, arrived_held))
            for at in range(col_count // 2)
        ])

    carrier = local - 2 if pair_bits == 1 else local
    again, near_again, sent, token, stats = [], [], [], None, None
    for first in range(local + 1):
        if first < local:
            slots = apart if first == local - 1 else joined
            tokens = ([token] if first else []) + ([near_again[-1]] if near_again else [])
            coded = [held, arrived_held] if first == carrier else []
            *sums, token = multiply(blocks, slots, first, tokens, coded)
            stats = token if coded else stats
            again.append(exchange(sums))
        for done in range(len(near_again), first if first < local else local):
            kept, arrived = again[done]
            tokens = [token] + (sent[done - 2:done - 1] if done > 1 else []) + (near_images[-1:] if done == 1 else [])
            if done == carrier:
                near, stats = emit(kept, arrived[-1], tokens, stats)
            else:
                (near,) = emit(kept, arrived[-1], tokens)
            near_again.append(near)
            sent.append(to_partner(near))
    if carrier == local:
        stats = settle(held, arrived_held, [token])
        for bit in range(pair_bits):
            stats = stats + lax.ppermute(stats, both, leader_swap(1 << bit))
        stats = jnp.where(leading, stats, to_partner(stats))
    return tuple(finish(entry_count, carrier, stats, [part[0] for part in parts], near_images, again, sent, [arrive(2 * 10**9, *sent[:-1])]))


def solution(mesh):
    placed = (
        P(("groups", "row"), "col"),
        P(None, ("groups", "row"), None, None),
        P(None, ("groups", "col"), None, None),
        P(None, "groups"),
        P(None, "groups"),
        P("groups"),
        P("groups"),
    )
    return jax.shard_map(
        on_device,
        mesh=mesh,
        in_specs=placed,
        out_specs=(P(("groups", "row"), "col"), P(("groups", "row"), "col")),
        check_vma=False,
    )
```

```python
import functools

import jax
import jax.numpy as jnp
from jax import lax
from jax.experimental import pallas as pl
from jax.experimental.pallas import tpu as pltpu
from jax.sharding import PartitionSpec as P

MIB = 1024 * 1024
CODE_ROWS = 16
VMEM_LIMIT = 10 * MIB
MASK_LIMIT = 60 * MIB
ANY = pl.BlockSpec(memory_space=pl.ANY)
BRIEF = pl.CostEstimate(flops=10**9, bytes_accessed=0, transcendentals=0)
TOKEN = jax.ShapeDtypeStruct((2, 8, 128), jnp.float32)
VMEM = pl.BlockSpec(memory_space=pltpu.VMEM)
SMEM = pl.BlockSpec(memory_space=pltpu.SMEM)


def bits_of(size):
    count = size.bit_length() - 1
    assert 1 << count == size
    return count


def swap(axis, bit):
    return [(place, place ^ bit) for place in range(lax.axis_size(axis))]


def leads(row):
    return (row ^ (row >> 1)) & 1


def leader_swap(bit):
    rows, cols = lax.axis_size("row"), lax.axis_size("col")
    pairs = []
    for row in range(rows):
        for col in range(cols):
            if leads(row):
                pair = (row >> 1) ^ bit
                there = (2 * pair if leads(2 * pair) else 2 * pair + 1, col)
            else:
                there = (row, col ^ 1)
            pairs.append((row * cols + col, there[0] * cols + there[1]))
    return pairs


def reverse_bits(value, count):
    out = 0
    for bit in range(count):
        out = out | (((value >> bit) & 1) << (count - 1 - bit))
    return out


def keep_corner(block, rows, cols):
    inside = (lax.broadcasted_iota(jnp.int32, block.shape, 0) < rows) & (
        lax.broadcasted_iota(jnp.int32, block.shape, 1) < cols
    )
    return jnp.where(inside, block.astype(jnp.float32), 0.0).astype(block.dtype)


def mask_left_kernel(left_dest, left_sizes, left, out, near, token):
    token[...] = jnp.zeros_like(token)
    row, col = lax.axis_index("row"), lax.axis_index("col")
    terms, half = out.shape[0], near.shape[0]
    for term in range(terms):
        out[term] = keep_corner(left[term, 0], left_sizes[left_dest[term, row]], left_sizes[row])
    for place in range(half):
        near[place] = out[lax.rem(col, 2) * half + place]


def mask_left(left_dest, left_sizes, left):
    terms, _, tile, _ = left.shape
    return pl.pallas_call(
        mask_left_kernel,
        in_specs=[SMEM, SMEM, VMEM],
        out_specs=[VMEM] * 3,
        out_shape=[jax.ShapeDtypeStruct((count, tile, tile), left.dtype) for count in (terms, terms // 2)] + [TOKEN],
        compiler_params=pltpu.CompilerParams(vmem_limit_bytes=MASK_LIMIT),
        cost_estimate=BRIEF,
    )(left_dest, left_sizes, left)


def mask_right_kernel(right_src, right_sizes, right, *outs):
    *outs, token = outs
    token[...] = jnp.zeros_like(token)
    col = lax.axis_index("col")
    for step in range(right.shape[0]):
        term = pl.program_id(0) * right.shape[0] + step
        for place, out in enumerate(outs):
            block = col * len(outs) + place
            out[step] = keep_corner(right[step, place], right_sizes[block], right_sizes[right_src[term, block]])


def mask_right(right_src, right_sizes, right):
    terms, local, tile, _ = right.shape
    return pl.pallas_call(
        mask_right_kernel,
        grid=(terms // 2,),
        in_specs=[SMEM, SMEM, pl.BlockSpec((2, local, tile, tile), lambda step: (step, 0, 0, 0))],
        out_specs=[pl.BlockSpec((2, tile, tile), lambda step: (step, 0, 0))] * local
        + [pl.BlockSpec(TOKEN.shape, lambda step: (0, 0, 0))],
        out_shape=[jax.ShapeDtypeStruct((terms, tile, tile), right.dtype)] * local + [TOKEN],
        compiler_params=pltpu.CompilerParams(vmem_limit_bytes=MASK_LIMIT),
        cost_estimate=BRIEF,
    )(right_src, right_sizes, right)


def place_kernel(places, *refs):
    pieces, (blocks, sems) = refs[:len(places)], refs[-2:]
    tile = blocks.shape[2]
    copies = []

    def add(here, there):
        copies.append(pltpu.make_async_copy(here, there, sems.at[len(copies)]))

    for (block, slot), piece in zip(places, pieces):
        if len(piece.shape) == 3:
            add(piece.at[:, :blocks.shape[1]], blocks.at[block:block + piece.shape[0]])
        else:
            for at in range(piece.shape[1] // tile):
                rows = piece.shape[0]
                add(piece.at[:, at * tile:(at + 1) * tile], blocks.at[block + at, slot * tile:slot * tile + rows])
    for copy in copies:
        copy.start()
    for copy in copies:
        copy.wait()


def place(blocks, shape, pieces, tokens=()):
    places, pieces = [at for at, _ in pieces], [piece for _, piece in pieces]
    copies = sum(1 if piece.ndim == 3 else piece.shape[1] // shape[2] for piece in pieces)
    rest = list(tokens) if blocks is None else [blocks, *tokens]
    return pl.pallas_call(
        functools.partial(place_kernel, places),
        in_specs=[ANY] * (len(pieces) + len(rest)),
        out_specs=ANY,
        out_shape=jax.ShapeDtypeStruct(shape, jnp.bfloat16),
        scratch_shapes=[pltpu.SemaphoreType.DMA((copies,))],
        input_output_aliases={} if blocks is None else {len(pieces): 0},
        compiler_params=pltpu.CompilerParams(vmem_limit_bytes=VMEM_LIMIT),
        cost_estimate=BRIEF,
    )(*pieces, *rest)


def join_kernel(*refs):
    held, pieces = refs[-1], refs[:refs[-1].shape[0]]
    rows = held.shape[1] - CODE_ROWS
    sums = [jnp.zeros((1, 1), jnp.float32)] * 2
    for at, piece in enumerate(pieces):
        held[at, :rows] = piece[:rows]
        sums = [total + more for total, more in zip(sums, decode(piece[rows:]))]
        if at:
            held[at, rows:] = jnp.zeros((CODE_ROWS, held.shape[2]), held.dtype)
    held[0, rows:] = encode(sums)


def join(pieces, tokens):
    return pl.pallas_call(
        join_kernel,
        in_specs=[VMEM] * len(pieces) + [ANY] * len(tokens),
        out_specs=VMEM,
        out_shape=jax.ShapeDtypeStruct((len(pieces), *pieces[0].shape), pieces[0].dtype),
        compiler_params=pltpu.CompilerParams(vmem_limit_bytes=VMEM_LIMIT),
        cost_estimate=BRIEF,
    )(*pieces, *tokens)


def read_codes(arrays, codes, sems):
    copies = [
        pltpu.make_async_copy(ref.at[0, ref.shape[1] - CODE_ROWS:], codes.at[at], sems.at[at])
        for at, ref in enumerate(arrays)
    ]
    for copy in copies:
        copy.start()
    for copy in copies:
        copy.wait()
    return jnp.stack([jnp.broadcast_to(sum(pair), (8, 128)) for pair in zip(decode(codes[0]), decode(codes[1]))])


def settle_kernel(held, arrived, *refs):
    out, codes, sems = refs[-3:]
    out[...] = read_codes((held, arrived), codes, sems)


def settle(held, arrived, tokens):
    return pl.pallas_call(
        settle_kernel,
        in_specs=[ANY] * (2 + len(tokens)),
        out_specs=VMEM,
        out_shape=jax.ShapeDtypeStruct((2, 8, 128), jnp.float32),
        scratch_shapes=[pltpu.VMEM((2, CODE_ROWS, held.shape[2]), held.dtype), pltpu.SemaphoreType.DMA((2,))],
        compiler_params=pltpu.CompilerParams(vmem_limit_bytes=VMEM_LIMIT),
        cost_estimate=BRIEF,
    )(held, arrived, *tokens)


def product_kernel(first, local, out_slots, coded, source, target, blocks, left_own, left_near, left_far, right, *refs):
    outs, (token, inner, total, held_right, sem, codes, code_sems) = refs[-7 - len(out_slots):-7], refs[-7:]
    pair_count = total.shape[0] // 2
    if coded:
        token[...] = read_codes(refs[:2], codes, code_sems)
    else:
        token[...] = jnp.zeros_like(token)
    copy = pltpu.make_async_copy(right, held_right, sem)
    copy.start()
    total[...] = jnp.zeros_like(total)
    copy.wait()
    terms, tile = right.shape[:2]
    row, col = lax.axis_index("row"), lax.axis_index("col")
    for term in range(terms):
        wanted = source[term, col * local + first]
        place_of = lax.bitwise_xor(lax.div(wanted, local), col)
        place_of = (place_of >> 1) + (place_of & 1) * (blocks.shape[0] // local // 2)
        held = place_of * local + lax.rem(wanted, local)
        inner[term] = lax.dot_general(
            blocks[held], held_right[term], (((1,), (1,)), ((), ())), preferred_element_type=jnp.float32
        ).astype(jnp.bfloat16)

    def add(left, term, slot):
        to = target[term, lax.bitwise_xor(row, slot)]
        to_slot = 2 * reverse_bits((to >> 1) ^ (row >> 1), bits_of(pair_count)) + 1 - leads(to)
        total[to_slot] += jnp.dot(left, inner[term, slot * tile:(slot + 1) * tile], preferred_element_type=jnp.float32)

    half = terms // 2
    near = lax.rem(col, 2) * half
    for term in range(terms):
        add(left_own[term], term, 0)
    for step in range(half):
        add(left_near[step], near + step, 1)
        add(left_far[step], half - near + step, 1)
    for slots, out in zip(out_slots, outs):
        for at, slot in enumerate(slots):
            out[at * tile:(at + 1) * tile] = total[slot].astype(out.dtype)
        if coded and slots[0] >= 2:
            out[len(slots) * tile:] = encode([token[0, :1, :1], token[1, :1, :1]])


def products(blocks, left, right, source, target, out_slots, first, tokens, coded=()):
    local, (terms, tile) = len(right), right[0].shape[:2]
    out_shape = [
        jax.ShapeDtypeStruct((len(slots) * tile + CODE_ROWS, tile), jnp.bfloat16)
        if coded and slots[0] >= 2
        else jax.ShapeDtypeStruct((len(slots) * tile, tile), jnp.bfloat16 if slots[0] >= 2 else jnp.float32)
        for slots in out_slots
    ] + [TOKEN]
    held = 2 * blocks.size + 8 * terms * tile * tile + sum(8 * out.size for out in out_shape)
    return pl.pallas_call(
        functools.partial(product_kernel, first, local, out_slots, bool(coded)),
        in_specs=[SMEM, SMEM] + [VMEM] * 4 + [ANY] * (1 + len(coded) + len(tokens)),
        out_specs=[VMEM] * (len(out_slots) + 1),
        out_shape=out_shape,
        scratch_shapes=[
            pltpu.VMEM((terms, 2 * tile, tile), jnp.bfloat16),
            pltpu.VMEM((sum(len(slots) for slots in out_slots), tile, tile), jnp.float32),
            pltpu.VMEM((terms, tile, tile), jnp.bfloat16),
            pltpu.SemaphoreType.DMA,
            pltpu.VMEM((2, CODE_ROWS, tile), jnp.bfloat16),
            pltpu.SemaphoreType.DMA((2,)),
        ],
        compiler_params=pltpu.CompilerParams(vmem_limit_bytes=held + 4 * MIB),
        cost_estimate=BRIEF,
    )(source, target, blocks, *left, right[first], *coded, *tokens)


def encode(values):
    rows = lax.broadcasted_iota(jnp.int32, (CODE_ROWS, 256), 0)
    out = jnp.zeros((CODE_ROWS, 256), jnp.float32)
    for at, value in enumerate(values):
        rest = jnp.broadcast_to(value, out.shape)
        for part in range(3):
            head = rest.astype(jnp.bfloat16).astype(jnp.float32)
            out = jnp.where(rows == 3 * at + part, head, out)
            rest = rest - head
    return out.astype(jnp.bfloat16)


def decode(code):
    code = code[:6, :1].astype(jnp.float32)
    return [code[at:at + 1] + code[at + 1:at + 2] + code[at + 2:at + 3] for at in (0, 3)]


def combine_kernel(first, local, left_sizes, right_sizes, kept, arrived, blocks, *refs):
    before = refs[0]
    both, near, stats, held, sem = refs[-5:]
    tile = near.shape[0]
    copy = pltpu.make_async_copy(blocks.at[first], held, sem)
    copy.start()
    row, col = lax.axis_index("row"), lax.axis_index("col")
    image = kept[...] + arrived[...].astype(jnp.float32)
    both[:2 * tile] = image.astype(both.dtype)
    near[...] = image[tile:].astype(near.dtype)
    copy.wait()
    norm = correlation = jnp.zeros((8, tile), jnp.float32)
    for slot in range(2):
        rows = pl.ds(slot * tile, tile)
        masked = keep_corner(held[rows], left_sizes[lax.bitwise_xor(row, slot)], right_sizes[col * local + first])
        masked = masked.astype(jnp.float32)
        norm += jnp.sum((masked * masked).reshape(-1, 8, tile), 0)
        correlation += jnp.sum((masked * image[slot * tile:(slot + 1) * tile]).reshape(-1, 8, tile), 0)
    if first:
        norm, correlation = norm + before[0], correlation + before[1]
    stats[0] = norm
    stats[1] = correlation
    if first == local - 1:
        both[2 * tile:] = encode([jnp.sum(norm), jnp.sum(correlation)])


def combine(first, local, left_sizes, right_sizes, kept, arrived, blocks, stats, tokens):
    tile = kept.shape[1]
    rows = 2 * tile + CODE_ROWS * (first == local - 1)
    more = ([stats] if first else []) + tokens
    return pl.pallas_call(
        functools.partial(combine_kernel, first, local),
        in_specs=[SMEM, SMEM, VMEM, VMEM, ANY] + ([VMEM] if first else []) + [ANY] * len(tokens),
        out_specs=[VMEM] * 3,
        out_shape=[jax.ShapeDtypeStruct((height, tile), arrived.dtype) for height in (rows, tile)]
        + [jax.ShapeDtypeStruct((2, 8, tile), jnp.float32)],
        scratch_shapes=[pltpu.VMEM((2 * tile, tile), blocks.dtype), pltpu.SemaphoreType.DMA],
        compiler_params=pltpu.CompilerParams(vmem_limit_bytes=VMEM_LIMIT),
        cost_estimate=BRIEF,
    )(left_sizes, right_sizes, kept, arrived, blocks, *more)


def emit_kernel(start, coded, kept, arrived, *refs):
    outs = refs[-1 - coded:]
    tile = kept.shape[1]
    outs[0][:tile] = (kept[tile:] + arrived[start:start + tile].astype(jnp.float32)).astype(outs[0].dtype)
    if coded:
        more = decode(arrived[arrived.shape[0] - CODE_ROWS:])
        stats = [refs[0][at, :1, :1] + more[at] for at in range(2)]
        outs[0][tile:] = encode(stats)
        for at, value in enumerate(stats):
            outs[1][at] = jnp.broadcast_to(value, outs[1].shape[1:])


def emit(kept, arrived, tokens, stats=None):
    tile, coded = kept.shape[1], stats is not None
    start = tile if arrived.shape[0] >= 2 * tile else 0
    return pl.pallas_call(
        functools.partial(emit_kernel, start, coded),
        in_specs=[VMEM] * (2 + coded) + [ANY] * len(tokens),
        out_specs=[VMEM] * (1 + coded),
        out_shape=[jax.ShapeDtypeStruct((tile + CODE_ROWS * coded, tile), arrived.dtype)] + [TOKEN] * coded,
        compiler_params=pltpu.CompilerParams(vmem_limit_bytes=VMEM_LIMIT),
        cost_estimate=BRIEF,
    )(kept, arrived, *([stats] if coded else []), *tokens)


def finish_kernel(entry_count, local, carrier, firsts, stats, *refs):
    parts, near_images, kept, arrived, near_again = (refs[at * local:(at + 1) * local] for at in range(5))
    *outs, scales = refs[-10:-7]
    image_held, kept_held, more_held, out_held, code, sems, out_sems = refs[-7:]
    tile = image_held.shape[1]
    leading = leads(lax.axis_index("row")) == 1

    def own(first):
        pairs = [(parts, image_held), (arrived, more_held), (kept, kept_held)]
        return [
            pltpu.make_async_copy(source[first].at[:tile], held.at[first], sems.at[at, first])
            for at, (source, held) in enumerate(pairs)
        ]

    def sent(first):
        pairs = [(near_images, image_held), (near_again, more_held)]
        copies = [
            pltpu.make_async_copy(source[first].at[:tile], held.at[first], sems.at[at, first])
            for at, (source, held) in enumerate(pairs)
        ]
        if first == carrier:
            copies.append(pltpu.make_async_copy(near_again[first].at[tile:], code, sems.at[2, first]))
        return copies

    def each(firsts, act):
        for first in firsts:
            @pl.when(leading)
            def _():
                for copy in own(first):
                    act(copy)

            @pl.when(jnp.logical_not(leading))
            def _():
                for copy in sent(first):
                    act(copy)

    order = sorted(firsts, key=lambda first: first != carrier)
    each(order, lambda copy: copy.start())
    scale = theta = None
    out_copies = []
    for first in order:
        each([first], lambda copy: copy.wait())
        if scale is None:
            scale, theta = stats[0, :1, :1], stats[1, :1, :1]
            if 0 in firsts:
                norm, correlation = scale, theta
                if carrier < local:
                    norm, correlation = (
                        jnp.where(leading, mine, theirs) for mine, theirs in zip((norm, correlation), decode(code[...]))
                    )
                scale = lax.rsqrt(norm / entry_count + 1e-06)
                theta = correlation / norm
            for at, value in enumerate((scale, theta)):
                scales[at] = jnp.broadcast_to(value, scales.shape[1:])
        image = image_held[first].astype(jnp.float32)
        value = jnp.where(leading, kept_held[first], 0.0) + more_held[first].astype(jnp.float32)
        out_held[0, first] = (image * scale).astype(out_held.dtype)
        out_held[1, first] = ((value - theta * image) * scale).astype(out_held.dtype)
        for at, out in enumerate(outs):
            copy = pltpu.make_async_copy(
                out_held.at[at, first], out.at[:, first * tile:(first + 1) * tile], out_sems.at[at, first]
            )
            copy.start()
            out_copies.append(copy)
    for copy in out_copies:
        copy.wait()


def finish(entry_count, carrier, firsts, stats, parts, near_images, again, near_again, tokens, outs=()):
    local, tile = len(parts), near_images[0].shape[0]
    out = jax.ShapeDtypeStruct((tile, local * tile), near_images[0].dtype)
    block = (local, tile, tile)
    return pl.pallas_call(
        functools.partial(finish_kernel, entry_count, local, carrier, firsts),
        in_specs=[VMEM] + [ANY] * (5 * local + len(outs) + len(tokens)),
        out_specs=[ANY, ANY, VMEM],
        out_shape=[out, out, TOKEN],
        input_output_aliases={5 * local + 1 + at: at for at in range(len(outs))},
        scratch_shapes=[
            pltpu.VMEM(block, out.dtype),
            pltpu.VMEM(block, jnp.float32),
            pltpu.VMEM(block, out.dtype),
            pltpu.VMEM((2, *block), out.dtype),
            pltpu.VMEM((CODE_ROWS, tile), out.dtype),
            pltpu.SemaphoreType.DMA((3, local)),
            pltpu.SemaphoreType.DMA((2, local)),
        ],
        compiler_params=pltpu.CompilerParams(vmem_limit_bytes=VMEM_LIMIT),
        cost_estimate=BRIEF,
    )(stats, *parts, *near_images, *(kept for kept, _ in again), *(arrived[0] for _, arrived in again), *near_again, *outs, *tokens)


def after_kernel(value, *refs):
    refs[-1][...] = value[...]


def after(value, *others):
    return pl.pallas_call(
        after_kernel,
        in_specs=[VMEM] + [ANY] * len(others),
        out_specs=VMEM,
        out_shape=jax.ShapeDtypeStruct(value.shape, value.dtype),
        compiler_params=pltpu.CompilerParams(vmem_limit_bytes=VMEM_LIMIT),
        cost_estimate=BRIEF,
    )(value, *others)


def arrive_kernel(*refs):
    refs[-1][...] = jnp.zeros_like(refs[-1])


def arrive(cost, *values):
    return pl.pallas_call(
        arrive_kernel,
        in_specs=[ANY] * len(values),
        out_specs=VMEM,
        out_shape=TOKEN,
        compiler_params=pltpu.CompilerParams(vmem_limit_bytes=VMEM_LIMIT),
        cost_estimate=pl.CostEstimate(flops=cost, bytes_accessed=0, transcendentals=0),
    )(*values)


def on_device(wavefunction, left_ops, right_ops, left_dest, right_src, left_sizes, right_sizes):
    tile = left_ops.shape[2]
    local = right_ops.shape[1]
    row_count, col_count = lax.axis_size("row"), lax.axis_size("col")
    pair_bits, col_bits = bits_of(row_count) - 1, bits_of(col_count)
    entry_count = wavefunction.shape[0] * row_count * wavefunction.shape[1] * col_count
    both = ("row", "col")
    row, col = lax.axis_index("row"), lax.axis_index("col")
    leading = leads(row) == 1
    blocks_shape = (col_count * local, 2 * tile, tile)

    def far(part):
        pieces = [part]
        for bit in range(1, col_bits):
            pieces += [lax.ppermute(piece, "col", swap("col", 1 << bit)) for piece in pieces]
        return pieces

    def other_core(part):
        return lax.ppermute(part, "col", swap("col", 1))

    def block_of(piece, odd):
        return (odd * (col_count // 2) + piece) * local

    def to_partner(part):
        return lax.ppermute(part, "row", swap("row", 1))

    near = to_partner(wavefunction)
    left_own, left_near, left_token = mask_left(left_dest, left_sizes, left_ops)
    left_near = to_partner(left_near)
    left = [left_own, left_near, other_core(left_near)]
    *right, right_token = mask_right(right_src, right_sizes, right_ops)
    near = after(near, left_token, right_token)

    def exchange(sums):
        kept, sums = sums[0], sums[1:]
        per_pair = len(sums) // ((1 << pair_bits) - 1)
        for bit in range(pair_bits):
            half = (len(sums) + per_pair) // 2 - per_pair
            arrived = [lax.ppermute(part, both, leader_swap(1 << bit)) for part in sums[half:][::-1]][::-1]
            if bit < pair_bits - 1:
                mine = arrived[0] if per_pair == 1 else jnp.concatenate(arrived[:per_pair], 0)
                kept = kept + mine.astype(jnp.float32)
                sums = [
                    (part.astype(jnp.float32) + more.astype(jnp.float32)).astype(part.dtype)
                    for part, more in zip(sums[:half], arrived[per_pair:])
                ]
        return kept, arrived

    joined = [(2 * pair, 2 * pair + 1) for pair in range(1 << pair_bits)]
    apart = joined[:1] + [(slot,) for pair in joined[1:] for slot in pair]

    def multiply(blocks, slots, first, tokens, coded=()):
        return products(blocks, left, right, right_src, left_dest, slots, first, tokens, coded)

    left_there = arrive(2 * 10**9, left[2])

    pieces = [((block_of(at, 0), 0), piece) for at, piece in enumerate(far(wavefunction))]
    near_pieces = [((block_of(at, 0), 1), piece) for at, piece in enumerate(far(near))]
    blocks = None
    for several in (pieces + near_pieces[:1], near_pieces[1:]):
        blocks = place(blocks, blocks_shape, several + [
            ((block + block_of(0, 1), slot), other_core(piece)) for (block, slot), piece in several
        ])

    once, parts, near_images, stats, token = [], [], [], None, None
    for first in range(local + 1):
        if first < local:
            *sums, token = multiply(blocks, joined, first, ([token] if first else [left_there]) + ([stats] if parts else []))
            once.append(exchange(sums))
        for done in range(len(parts), first if first < local else local):
            kept, (arrived,) = once[done]
            image, near_image, stats = combine(
                done, local, left_sizes, right_sizes, kept, arrived, blocks, stats,
                [token] + (parts[0][1:] if done > 1 else []),
            )
            parts.append(far(image))
            near_images.append(to_partner(near_image))
    blocks = None
    for group in (range(local - 1), range(local - 1, local)):
        if blocks is None:
            held = place(
                None,
                (len(group) * col_count // 2, 2 * tile, tile),
                [((at * len(group) + i, 0), parts[first][at]) for at in range(col_count // 2) for i, first in enumerate(group)],
                [parts[-1][0], *near_images[:-2]],
            )
        else:
            held = join(parts[-1], [blocks, near_images[-2]])
        arrived_held = other_core(held)
        blocks = place(blocks, blocks_shape, [
            ((block_of(at, odd) + group[0], 0), half[at * len(group):(at + 1) * len(group)])
            for odd, half in enumerate((held, arrived_held))
            for at in range(col_count // 2)
        ])

    carrier = local - 2 if pair_bits == 1 else local
    again, near_again, sent, token, stats = [], [], [], None, None
    for first in range(local + 1):
        if first < local:
            slots = apart if first == local - 1 else joined
            tokens = ([token] if first else []) + ([near_again[-1]] if near_again else [])
            coded = [held, arrived_held] if first == carrier else []
            *sums, token = multiply(blocks, slots, first, tokens, coded)
            stats = token if coded else stats
            again.append(exchange(sums))
        for done in range(len(near_again), first if first < local else local):
            kept, arrived = again[done]
            tokens = [token] + (sent[done - 2:done - 1] if done > 1 else []) + (near_images[-1:] if done == 1 else [])
            if done == carrier:
                near, stats = emit(kept, arrived[-1], tokens, stats)
            else:
                (near,) = emit(kept, arrived[-1], tokens)
            near_again.append(near)
            sent.append(to_partner(near))
    if carrier == local:
        stats = settle(held, arrived_held, [token])
        for bit in range(pair_bits):
            stats = stats + lax.ppermute(stats, both, leader_swap(1 << bit))
        stats = jnp.where(leading, stats, to_partner(stats))
    images = [part[0] for part in parts]
    last = local - 1
    early = [*sent[:last], sent[0]]
    *outs, scales = finish(
        entry_count, carrier, list(range(last)), stats, images, near_images, again[:last] + again[:1], early,
        [arrive(2 * 10**9, *sent[:last])],
    )
    *outs, _ = finish(entry_count, carrier, [last], scales, images, near_images, again, sent, [], outs)
    return tuple(outs)


def solution(mesh):
    placed = (
        P(("groups", "row"), "col"),
        P(None, ("groups", "row"), None, None),
        P(None, ("groups", "col"), None, None),
        P(None, "groups"),
        P(None, "groups"),
        P("groups"),
        P("groups"),
    )
    return jax.shard_map(
        on_device,
        mesh=mesh,
        in_specs=placed,
        out_specs=(P(("groups", "row"), "col"), P(("groups", "row"), "col")),
        check_vma=False,
    )
```
